256 devices in a mesh: fsdp: 32 (over z, x_lo, core), tenant: 4 (over y), tensor: 2 (over x_hi).
Axes of the slice: x: 4 (x_hi: 2, x_lo: 2; x = x_hi * 2 + x_lo), y: 4, z: 8, core: 2. Of those that a mesh axis runs over, the one named last changes fastest.
Arguments:
- tokens: bfloat16 [16384, 8192], P(('fsdp', 'tenant')), may hold values from -6 to 6
- inner_x: bfloat16 [16384, 8192], P(('fsdp', 'tenant'), 'tensor'), may hold values from -6 to 6
- step_size: float32 [16384, 128], P(('fsdp', 'tenant'), 'tensor'), may hold values from 0.01 to 0.25
- decay_rate: float32 [128], P('tensor'), may hold values from 0.2 to 16
- grad_out: bfloat16 [16384, 8192], P(('fsdp', 'tenant'), 'tensor'), may hold values from -6 to 6
- w_bc: bfloat16 [8192, 2048], P('fsdp', 'tensor'), may hold values from -0.0625 to 0.0625
- a_store: bfloat16 [256, 8192, 64], P(('fsdp', 'tenant'), 'tensor'), may hold values from -0.0625 to 0.0625
- b_store: bfloat16 [256, 64, 2048], P(('fsdp', 'tenant'), None, 'tensor'), may hold values from -0.75 to 0.75
- tenant_list: int32 [4, 2], P('tenant'), may hold values from 0 to 255, as said below
- block_slot: int32 [128], P(('fsdp', 'tenant')), may hold values from 0 to 1, as said below
- owner_slot: int32 [256], replicated, may hold values from 0 to 255, as said below
Outputs:
- mixed_out: bfloat16 [16384, 8192], P(('fsdp', 'tenant'), 'tensor')
- input_grad: bfloat16 [16384, 8192], P(('fsdp', 'tenant'), 'tensor')
- a_grad: bfloat16 [256, 8192, 64], P(('fsdp', 'tenant'), 'tensor')
- b_grad: bfloat16 [256, 64, 2048], P(('fsdp', 'tenant'), None, 'tensor')
The draws below stay inside these ranges and needn't reach their ends.
Inputs may be any that keep to these rules, and one draw needn't show every extreme that they name: `tenant_list`: row g lists the tenants of data group g; entries of a row are distinct. `block_slot`: sample b belongs to data group (b) mod 4. In each group the positions used are 0 up to some count, each used by some sample; the count is 2 in some group. Tenant t's adapters are row owner_slot[t] of a_store and b_store; every row belongs to exactly one tenant. The row owner_slot[tenant_list[g, j]] lies on the devices of tenant index (g + 2 - j) mod 4.
All inputs are finite; a program needn't handle non-finite values.
Results may differ from the reference program's by a relative error of at most 0.012.
Values may be sent and summed in bfloat16 or wider, within the bound.
A program may use at most 320 MiB of HBM per device.

```python
import math
import jax
import jax.numpy as jnp
from jax import lax

D = 8192
HEADS_GRP = 32
NS = 256
R = 64
TEN = 256
LIST_MAX = 2
BLK = 128
HEADS = 128
CH = 8192
BCW = 2048
GROUPS = 4
OWN = 2
BLOCKS_DEV = 1
TOKENS = 16384
NBLK = 128


def move_tenant(perm, tenant_id, slot):
    index = jnp.arange(TEN, dtype=jnp.int32)
    holder = jnp.sum(jnp.where(perm == slot, index, 0)).astype(jnp.int32)
    moved = jnp.where(index == holder, perm[tenant_id], perm)
    return jnp.where(index == tenant_id, slot, moved).astype(jnp.int32)


def shared_lists(key):
    base = jax.random.fold_in(key, 11)
    key_count, key_full, key_perm, key_pick, key_fsdp, key_own = jax.random.split(base, 6)
    counts = jax.random.randint(key_count, (GROUPS,), 1, LIST_MAX + 1)
    fullest = jax.random.randint(key_full, (), 0, GROUPS)
    counts = jnp.where(jnp.arange(GROUPS) == fullest, LIST_MAX, counts)
    fsdp_count = TEN // (GROUPS * OWN)
    group_idx = jnp.arange(GROUPS)[:, None]
    position = jnp.arange(LIST_MAX)[None, :]
    target = (group_idx + 2 - position) % GROUPS
    fsdp_pick = jax.random.randint(key_fsdp, (GROUPS, LIST_MAX), 0, fsdp_count)
    own_pick = jax.random.randint(key_own, (GROUPS, LIST_MAX), 0, OWN)
    slots = ((fsdp_pick * GROUPS + target) * OWN + own_pick).astype(jnp.int32)
    perm = jax.random.permutation(key_perm, TEN).astype(jnp.int32)
    second = (fullest + 1) % GROUPS
    perm = move_tenant(perm, 0, slots[second, 0])
    perm = move_tenant(perm, TEN - 1, slots[fullest, 0])
    inverse = jnp.zeros((TEN,), jnp.int32).at[perm].set(jnp.arange(TEN, dtype=jnp.int32))
    all_lists = inverse[slots].astype(jnp.int32)
    blocks = jnp.arange(NBLK)
    device = blocks // BLOCKS_DEV
    group_of = device % GROUPS
    within = device // GROUPS * BLOCKS_DEV + blocks % BLOCKS_DEV
    limit_of = counts[group_of]
    noise_int = jax.random.randint(key_pick, (NBLK,), 0, 1048576)
    slot_ids = jnp.where(within < limit_of, within, noise_int % limit_of).astype(jnp.int32)
    return (all_lists, slot_ids, perm)


def draw_tenant_list(key, part):
    return shared_lists(key)[0]


def draw_block_slot(key, part):
    return shared_lists(key)[1]


def draw_owner_slot(key, part):
    return shared_lists(key)[2]


def levels(rng, dims, pieces, low, high):
    gain = 1.0
    for dim, parts in pieces:
        steps = jax.random.uniform(jax.random.fold_in(jax.random.fold_in(rng, 6), dim), (parts,), jnp.float32, low / len(pieces), high / len(pieces))
        gain = gain * jnp.repeat(jnp.exp(steps), dims[dim] // parts).reshape((-1,) + (1,) * (len(dims) - 1 - dim))
    return gain


def noise(stream_key, dims, scale, most, cuts=(), held_as=jnp.bfloat16):
    array = scale * jax.random.normal(stream_key, dims, jnp.float32)
    if cuts:
        array = array * levels(stream_key, dims, cuts, -0.22, 0.18)
    return jnp.clip(array, -most, most).astype(held_as)


def setup_inputs(seed: int = 0) -> dict:
    seeds = jax.random.split(jax.random.key(seed), 12)
    return {
        "tokens": noise(seeds[0], (TOKENS, D), 1.0, 6.0, ((0, 128),)),
        "inner_x": noise(seeds[1], (TOKENS, CH), 1.0, 6.0, ((0, 128), (1, 2))),
        "step_size": jnp.clip(jnp.exp(math.log(0.25) - 3.218876 * jax.random.uniform(seeds[2], (TOKENS, HEADS), jnp.float32) ** levels(seeds[2], (TOKENS, HEADS), ((0, 128), (1, 2)), -0.2, 0.2)), 0.01, 0.25),
        "decay_rate": jnp.clip(jnp.exp(math.log(16.0) - 4.3820266 * jax.random.uniform(seeds[3], (HEADS,), jnp.float32) ** levels(seeds[3], (HEADS,), ((0, 2),), -0.2, 0.2)), 0.2, 16.0),
        "grad_out": noise(seeds[4], (TOKENS, CH), 1.0, 6.0, ((0, 128), (1, 2))),
        "w_bc": noise(seeds[5], (D, BCW), D ** -0.5, 0.0625, ((0, 32), (1, 2))),
        "a_store": noise(seeds[6], (TEN, D, R), D ** -0.5, 0.0625, ((0, 128), (1, 2))),
        "b_store": noise(seeds[7], (TEN, R, BCW), R ** -0.5, 0.75, ((0, 128), (2, 2))),
        "tenant_list": draw_tenant_list(jax.random.fold_in(seeds[11], 71), 0),
        "block_slot": draw_block_slot(jax.random.fold_in(seeds[11], 71), 0),
        "owner_slot": draw_owner_slot(jax.random.fold_in(seeds[11], 71), 0),
    }


def mix_state(proj_in, inner_x, step_size, decay_rate, block_len, heads_grp, state_dim):
    length = proj_in.shape[0]
    nblock = length // block_len
    groups = proj_in.shape[1] // (2 * state_dim)
    num_heads = decay_rate.shape[0]
    head_dim = inner_x.shape[1] // num_heads
    split_proj = proj_in.reshape(nblock, block_len, groups, 2, state_dim)
    b_input = split_proj[:, :, :, 0, :]
    c_output = split_proj[:, :, :, 1, :]
    values = inner_x.astype(jnp.float32).reshape(nblock, block_len, groups, heads_grp, head_dim)
    step_blk = step_size.reshape(nblock, block_len, groups, heads_grp)
    log_decay = -step_blk * decay_rate.reshape(groups, heads_grp)
    totals = jnp.cumsum(log_decay, axis=1)
    spread = totals[:, :, None] - totals[:, None, :]
    causal = jnp.arange(block_len)[:, None] >= jnp.arange(block_len)[None, :]
    decay_mat = jnp.exp(jnp.where(causal[None, :, :, None, None], spread, -1e+30))
    scores = jnp.einsum('ntgk,nsgk->ntsg', c_output, b_input, precision=lax.Precision.HIGHEST)
    weight = decay_mat * scores[..., None] * step_blk[:, None]
    mixed_all = jnp.einsum('ntsgh,nsghp->ntghp', weight, values, precision=lax.Precision.HIGHEST)
    return mixed_all.reshape(length, num_heads * head_dim)

def reference(tokens, inner_x, step_size, decay_rate, grad_out, w_bc, a_store, b_store, tenant_list, block_slot, owner_slot):
    nblock = TOKENS // BLK
    device = jnp.arange(nblock, dtype=jnp.int32) // BLOCKS_DEV
    group_of = (device % GROUPS).astype(jnp.int32)
    tenant = tenant_list[group_of, block_slot]
    store_row = owner_slot[tenant].astype(jnp.int32)
    token_blocks = tokens.reshape(nblock, BLK, D)
    inner_blocks = inner_x.reshape(nblock, BLK, CH)
    step_blocks = step_size.reshape(nblock, BLK, HEADS)
    grad_blocks = grad_out.reshape(nblock, BLK, CH)

    def one_block(carried, element):
        grad_a, grad_b = carried
        block_tokens, block_inner, block_step, block_grad, block_row, block_group, block_pos = element
        a_mat = a_store[block_row]
        b_mat = b_store[block_row]
        low_rank = jnp.dot(block_tokens, a_mat, preferred_element_type=jnp.float32).astype(jnp.bfloat16)
        proj = (jnp.dot(block_tokens, w_bc, preferred_element_type=jnp.float32) + jnp.dot(low_rank, b_mat, preferred_element_type=jnp.float32)).astype(jnp.bfloat16)

        def mixer(proj_in):
            return mix_state(proj_in, block_inner, block_step, decay_rate, BLK, HEADS_GRP, NS)
        mixed_now, pull_back = jax.vjp(mixer, proj.astype(jnp.float32))
        grad_proj, = pull_back(block_grad.astype(jnp.float32))
        grad_proj = grad_proj.astype(jnp.bfloat16)
        q_low = jnp.dot(grad_proj, b_mat.T, preferred_element_type=jnp.float32).astype(jnp.bfloat16)
        input_now = (jnp.dot(grad_proj, w_bc.T, preferred_element_type=jnp.float32) + jnp.dot(q_low, a_mat.T, preferred_element_type=jnp.float32)).astype(jnp.bfloat16)
        grad_a = grad_a.at[block_group, block_pos].add(jnp.dot(block_tokens.T, q_low, preferred_element_type=jnp.float32))
        grad_b = grad_b.at[block_group, block_pos].add(jnp.dot(low_rank.T, grad_proj, preferred_element_type=jnp.float32))
        return ((grad_a, grad_b), (mixed_now.astype(jnp.bfloat16), input_now))
    start_a = jnp.zeros((GROUPS, LIST_MAX, D, R), jnp.float32)
    start_b = jnp.zeros((GROUPS, LIST_MAX, R, BCW), jnp.float32)
    (sum_a, sum_b), (outs_mixed, outs_input) = lax.scan(one_block, (start_a, start_b), (token_blocks, inner_blocks, step_blocks, grad_blocks, store_row, group_of, block_slot))
    group_a = lax.optimization_barrier(sum_a.astype(jnp.bfloat16)).astype(jnp.float32)
    group_b = lax.optimization_barrier(sum_b.astype(jnp.bfloat16)).astype(jnp.float32)
    targets = owner_slot[tenant_list].reshape(GROUPS * LIST_MAX).astype(jnp.int32)
    a_grad = jnp.zeros((TEN, D, R), jnp.float32).at[targets].add(group_a.reshape(GROUPS * LIST_MAX, D, R)).astype(jnp.bfloat16)
    b_grad = jnp.zeros((TEN, R, BCW), jnp.float32).at[targets].add(group_b.reshape(GROUPS * LIST_MAX, R, BCW)).astype(jnp.bfloat16)
    return (outs_mixed.reshape(TOKENS, CH), outs_input.reshape(TOKENS, D), a_grad, b_grad)
```

```python
import jax
import jax.numpy as jnp
from jax import lax
from jax.experimental import pallas as pl
from jax.experimental.pallas import tpu as pltpu
from jax.sharding import PartitionSpec as P

MESH = pl.DeviceIdType.MESH
F32 = jnp.float32
BF16 = jnp.bfloat16
NZ = 8
HEADS_GRP = 32
NS = 256

X_, Z_, Y_, D_ = 0, 2, 18, 34
LIST_, FCORE, FX, FZ_, FY, GZ_, GX, GCORE, LOW = 50, 52, 53, 54, 62, 63, 71, 72, 73
Q, PIN_, BCORE, BZ_, BX, BY, HX, HZ_, HCORE = 74, 75, 79, 80, 88, 89, 90, 91, 99
SLOTS = 100

NN = (((1,), (0,)), ((), ()))
NT = (((1,), (1,)), ((), ()))
TN = (((0,), (0,)), ((), ()))


def dot(a, b, dims=NN, precision=None):
    return lax.dot_general(a, b, dims, precision=precision, preferred_element_type=F32)


def body(
    slot_ref, tok_hbm, x_hbm, step_ref, rate_ref, g_hbm, w_hbm, a_hbm, b_hbm, loc_ref,
    mixed_hbm, igrad_hbm, agrad_hbm, bgrad_hbm,
    w, tok, x, g, a_own, b_own, listed, cand, rcore, rx, rz, chunk, ry, full,
    sel_a, sel_b, low_s, low_r, low_t, decay, tot, score_grad, acc, proj, gproj,
    q_s, q_r, q_t, psend, precv, part, mixed, igrad,
    bcand, brcore, brz, bs, brx, bchunk, bry, bfull, agrad, bgrad,
    ssem, rsem, lsem,
):
    f = lax.axis_index("fsdp")
    y = lax.axis_index("tenant")
    t = lax.axis_index("tensor")
    z = f // 4
    l = (f // 2) % 2
    c = f % 2
    p = y % 2
    rows = tok.shape[0]
    pairs = x.shape[1] // 128
    grp_pairs = pairs // 2

    def zat(d):
        return (z + d + NZ) % NZ

    def zdev(d):
        return (zat(d) * 4 + l * 2 + c, y, t)

    def ydev(d):
        return (f, (y + d + 4) % 4, t)

    sib = (z * 4 + l * 2 + (1 - c), y, t)
    xdev = (z * 4 + (1 - l) * 2 + c, y, t)
    tdev = (f, y, 1 - t)

    sent = []

    def send(src, dst, slot, dev):
        copy = pltpu.make_async_remote_copy(
            src_ref=src, dst_ref=dst, send_sem=ssem.at[slot], recv_sem=rsem.at[slot],
            device_id=dev, device_id_type=MESH,
        )
        copy.start()
        sent.append(copy)

    def got(dst, slot):
        pltpu.make_async_remote_copy(
            src_ref=dst, dst_ref=dst, send_sem=ssem.at[slot], recv_sem=rsem.at[slot],
            device_id=sib, device_id_type=MESH,
        ).wait_recv()

    def local(src, dst, slot):
        copy = pltpu.make_async_copy(src, dst, lsem.at[slot])
        copy.start()
        return copy

    def lside(which):
        return l if which == 0 else 1 - l

    def piece(d, which, par):
        first = pl.multiple_of((lside(which) * 2 + c) * 256 + par * 128, 128)
        return w.at[zat(d), pl.ds(first, 128), :]

    def whole(d, which, core):
        first = pl.multiple_of((lside(which) * 2 + core) * 256, 256)
        return w.at[zat(d), pl.ds(first, 256), :]

    load_w = local(w_hbm, whole(0, 0, c), 0)
    load_a = local(a_hbm, a_own, 1)
    load_b = local(b_hbm, b_own, 2)
    load_x = local(x_hbm, x, 3)
    load_g = local(g_hbm, g, 4)
    load_tok = local(tok_hbm, tok, 5)

    barrier = pltpu.get_barrier_semaphore()
    partners = [sib, xdev, tdev] + [zdev(d) for d in range(1, NZ)] + [ydev(d) for d in range(1, 4)]
    for dev in partners:
        pl.semaphore_signal(barrier, inc=1, device_id=dev, device_id_type=MESH)
    pl.semaphore_wait(barrier, len(partners))

    for j in range(2):
        send(loc_ref, listed.at[j], LIST_ + j, ydev(2 - j))
    load_w.wait()
    send(piece(0, 0, p), piece(0, 0, p), X_, xdev)
    for way in range(2):
        send(piece(0, 0, p), piece(0, 0, p), Z_ + way * 8, zdev(1 - 2 * way))
    send(piece(0, 0, 1 - p), piece(0, 0, 1 - p), X_ + 1, xdev)
    send(whole(0, 0, c), whole(0, 0, c), D_, sib)

    upto = (
        lax.broadcasted_iota(jnp.int32, (rows, rows), 0)
        <= lax.broadcasted_iota(jnp.int32, (rows, rows), 1)
    ).astype(F32)
    tot[...] = dot(-step_ref[...] * rate_ref[...], upto, precision=lax.Precision.HIGHEST)
    score_grad[...] = jnp.zeros_like(score_grad)
    load_x.wait()
    load_g.wait()

    lanes = lax.broadcasted_iota(jnp.int32, (rows, 128), 1)

    def split_heads(values):
        wide = values.astype(F32)
        one = jnp.where(lanes < 64, wide, 0.0).astype(BF16)
        two = jnp.where(lanes >= 64, wide, 0.0).astype(BF16)
        return jnp.concatenate([one, two], axis=0)

    def decay_pairs(first, count):
        causal = lax.broadcasted_iota(jnp.int32, (rows, rows), 0) >= lax.broadcasted_iota(
            jnp.int32, (rows, rows), 1
        )

        def one_pair(k, carry):
            at = pl.multiple_of(k * 128, 128)
            both = split_heads(x[:, pl.ds(at, 128)])
            outer = dot(g[:, pl.ds(at, 128)], both, NT)
            total = jnp.zeros((rows, rows), F32)
            for i in range(2):
                head = 2 * k + i
                along = jnp.broadcast_to(tot[pl.ds(head, 1), :], (rows, rows))
                spread = jnp.where(causal, along.T - along, -1e30)
                factor = jnp.exp(spread) * step_ref[pl.ds(head, 1), :]
                decay[head] = factor
                total += factor * outer[:, i * 128 : (i + 1) * 128]
            score_grad[k // grp_pairs] += total
            return carry

        lax.fori_loop(first, first + count, one_pair, 0)

    base = ((f * 4) + y) * 2
    for j in range(2):
        got(listed.at[j], LIST_ + j)

    def picked(j, k):
        return (listed[j, j : j + 1, :] == base + k).astype(F32)

    load_a.wait()
    load_b.wait()
    for j in range(2):
        m0, m1 = picked(j, 0), picked(j, 1)
        for zc in range(NZ):
            for i in range(5):
                src, at = (a_own, zc * 512 + i * 128) if i < 4 else (b_own, zc * 128)
                value = (
                    src[0, :, at : at + 128].astype(F32) * m0
                    + src[1, :, at : at + 128].astype(F32) * m1
                )
                cand[j, zc, :, i * 128 : (i + 1) * 128] = value.astype(BF16)
    send(cand.at[1 - c], rcore, FCORE, sib)

    got(piece(0, 1, p), X_)
    for way in range(2):
        send(piece(0, 1, p), piece(0, 1, p), Z_ + way * 8 + 4, zdev(1 - 2 * way))

    def zstep(s):
        for way, which, last in ((0, 0, 4), (1, 0, 3), (1, 1, 4), (0, 1, 3)):
            if s > last:
                continue
            d = -s if way == 0 else s
            slot = Z_ + way * 8 + which * 4 + s - 1
            part_in = piece(d, which, p)
            got(part_in, slot)
            if s < last:
                send(part_in, part_in, slot + 1, zdev(1 - 2 * way))
            send(part_in, part_in, Y_ + which * 8 + d % 8, ydev(1 if which == 0 else -1))

    def offsets(s):
        return (0,) if s == 0 else (4,) if s == 4 else (-s, s)

    def ystep(s):
        for d in offsets(s):
            for which in range(2):
                got(piece(d, which, 1 - p), Y_ + which * 8 + d % 8)
                send(whole(d, which, c), whole(d, which, c), D_ + which * 8 + d % 8, sib)

    def forward(s):
        for d in offsets(s):
            for which in range(2):
                got(whole(d, which, 1 - c), D_ + which * 8 + d % 8)
        for d in offsets(s):
            at = zat(d)

            def part_n(n, carry, at=at, first=s == 0):
                cols = pl.ds(pl.multiple_of(n * 256, 256), 256)
                value = dot(tok[:, pl.ds(pl.multiple_of(at * 1024, 1024), 1024)], w[at, :, cols])
                if first:
                    acc[:, cols] = value
                else:
                    acc[:, cols] += value
                return carry

            lax.fori_loop(0, 4, part_n, 0)

    quarter = pairs // 4
    decay_pairs(0, quarter)
    got(piece(0, 1, 1 - p), X_ + 1)
    send(whole(0, 1, c), whole(0, 1, c), D_ + 8, sib)
    zstep(1)

    got(rcore, FCORE)
    cand[c] = cand[c] + rcore[...]
    mine = pl.ds(pl.multiple_of(32 * l, 32), 32)
    other = pl.ds(pl.multiple_of(32 * (1 - l), 32), 32)
    send(cand.at[c, :, other, :], rx, FX, xdev)
    decay_pairs(quarter, quarter)
    load_tok.wait()
    forward(0)
    zstep(2)
    ystep(1)
    got(rx, FX)
    rx[...] = rx[...] + cand[c, :, mine, :]
    for d in range(1, NZ):
        send(rx.at[zat(d)], rz.at[d], FZ_ + d, zdev(d))
    decay_pairs(2 * quarter, quarter)
    forward(1)
    zstep(3)
    ystep(2)
    total = rx[z].astype(F32)
    for d in range(1, NZ):
        got(rz.at[d], FZ_ + d)
        total += rz[d].astype(F32)
    chunk[...] = total.astype(BF16)
    send(chunk, ry, FY, ydev(2 + c))
    decay_pairs(3 * quarter, quarter)
    forward(2)
    got(ry, FY)
    full[c, z, mine, :] = ry[...]
    for d in range(1, NZ):
        send(ry, full.at[c, z, mine, :], GZ_ + d, zdev(d))
    zstep(4)
    ystep(3)
    for d in range(1, NZ):
        got(full.at[c, zat(-d), mine, :], GZ_ + d)
    send(full.at[c, :, mine, :], full.at[c, :, mine, :], GX, xdev)
    forward(3)
    got(full.at[c, :, other, :], GX)
    send(full.at[c], full.at[c], GCORE, sib)
    ystep(4)
    got(full.at[1 - c], GCORE)
    slot = slot_ref[0]
    half = pl.multiple_of(t * 4096, 4096)
    low_part = jnp.zeros((64, rows), F32)
    for zc in range(NZ):
        piece_ab = full[slot, zc]
        sel_a[:, zc * 512 : (zc + 1) * 512] = piece_ab[:, :512]
        sel_b[:, zc * 128 : (zc + 1) * 128] = piece_ab[:, 512:]
        low_part += dot(piece_ab[:, :512], tok[:, pl.ds(half + zc * 512, 512)], NT)
    low_s[...] = low_part
    send(low_s, low_r, LOW, tdev)
    forward(4)
    got(low_r, LOW)
    low_t[...] = (low_s[...] + low_r[...]).astype(BF16)
    proj[...] = (acc[...] + dot(low_t[...], sel_b[...], TN)).astype(BF16)

    scores = []
    for gi in range(2):
        b_in = proj[:, gi * 512 : gi * 512 + 256]
        c_out = proj[:, gi * 512 + 256 : gi * 512 + 512]
        scores.append(dot(c_out, b_in, NT))
        sg = score_grad[gi].astype(BF16)
        gproj[:, gi * 512 : gi * 512 + 256] = dot(sg, c_out, TN).astype(BF16)
        gproj[:, gi * 512 + 256 : gi * 512 + 512] = dot(sg, b_in).astype(BF16)
    q_s[...] = dot(sel_b[...], gproj[...], NT)
    send(q_s, q_r, Q, tdev)
    for gi in range(2):
        score_grad[gi] = scores[gi]

    def back(at, n):
        return dot(gproj[...], w[at, pl.ds(pl.multiple_of(n * 256, 256), 256), :], NT)

    for k in range(4):

        def partner_n(n, carry, k=k):
            cols = pl.ds(pl.multiple_of(n * 256, 256), 256)
            psend[k, :, cols] = back(4 * (1 - t) + k, n).astype(BF16)
            return carry

        lax.fori_loop(0, 4, partner_n, 0)
        send(psend.at[k], precv.at[k], PIN_ + k, tdev)

    got(q_r, Q)
    q_t[...] = (q_s[...] + q_r[...]).astype(BF16)
    for zc in range(NZ):
        ga = dot(q_t[...], tok[:, pl.ds(half + zc * 512, 512)])
        gb = dot(low_t[...], gproj[:, zc * 128 : (zc + 1) * 128])
        for j in range(2):
            chosen = jnp.where(slot == j, 1.0, 0.0).astype(F32)
            bcand[j, zc, :, :512] = (ga * chosen).astype(BF16)
            bcand[j, zc, :, 512:] = (gb * chosen).astype(BF16)
    send(bcand.at[1 - c], brcore, BCORE, sib)

    def own_n(n, carry):
        cols = pl.ds(pl.multiple_of(n * 256, 256), 256)
        part[:, cols] = back(4 * t + n // 4, n % 4) + dot(q_t[...], sel_a[:, cols], TN)
        return carry

    lax.fori_loop(0, 16, own_n, 0)

    got(brcore, BCORE)
    for zc in range(NZ):
        bcand[c, zc] = (bcand[c, zc].astype(F32) + brcore[zc].astype(F32)).astype(BF16)
    for d in range(1, NZ):
        send(bcand.at[c, zat(d)], brz.at[d], BZ_ + d, zdev(d))

    def mix_pair(k, carry):
        at = pl.multiple_of(k * 128, 128)
        both = split_heads(x[:, pl.ds(at, 128)])
        score = score_grad[k // grp_pairs]
        weight = jnp.concatenate(
            [(decay[2 * k] * score).astype(BF16), (decay[2 * k + 1] * score).astype(BF16)], axis=1
        )
        mixed[:, pl.ds(at, 128)] = dot(weight, both).astype(BF16)
        return carry

    lax.fori_loop(0, pairs, mix_pair, 0)
    out_mixed = local(mixed, mixed_hbm, 6)

    total = bcand[c, z].astype(F32)
    for d in range(1, NZ):
        got(brz.at[d], BZ_ + d)
        total += brz[d].astype(F32)
    bs[...] = total.astype(BF16)
    send(bs.at[other, :], brx, BX, xdev)
    got(brx, BX)
    bchunk[...] = (bs[mine, :].astype(F32) + brx[...].astype(F32)).astype(BF16)
    send(bchunk, bry, BY, ydev(2 - c))
    got(bry, BY)
    bfull[c, z, mine, :] = bry[...]
    send(bry, bfull.at[c, z, mine, :], HX, xdev)
    got(bfull.at[c, z, other, :], HX)
    for d in range(1, NZ):
        send(bfull.at[c, z], bfull.at[c, z], HZ_ + d, zdev(d))

    for k in range(4):
        got(precv.at[k], PIN_ + k)
        cols = slice(k * 1024, (k + 1) * 1024)
        igrad[:, cols] = (part[:, cols] + precv[k].astype(F32)).astype(BF16)
    out_igrad = local(igrad, igrad_hbm, 7)

    for d in range(1, NZ):
        got(bfull.at[c, zat(-d)], HZ_ + d)
    send(bfull.at[c], bfull.at[c], HCORE, sib)
    got(bfull.at[1 - c], HCORE)
    for k in range(2):
        m0, m1 = picked(0, k), picked(1, k)
        for zc in range(NZ):
            for i in range(5):
                dst, at = (agrad, zc * 512 + i * 128) if i < 4 else (bgrad, zc * 128)
                lane = slice(i * 128, (i + 1) * 128)
                value = (
                    bfull[0, zc, :, lane].astype(F32) * m0 + bfull[1, zc, :, lane].astype(F32) * m1
                )
                dst[k, :, at : at + 128] = value.astype(BF16)
    out_a = local(agrad, agrad_hbm, 8)
    out_b = local(bgrad, bgrad_hbm, 9)
    for copy in sent:
        copy.wait_send()
    for copy in (out_mixed, out_igrad, out_a, out_b):
        copy.wait()


def shards(
    tokens, inner_x, step_size, decay_rate, grad_out, w_bc,
    a_store, b_store, tenant_list, block_slot, owner_slot,
):
    rows = tokens.shape[0]
    heads = decay_rate.shape[0]
    location = owner_slot[tenant_list[0]]
    loc = jnp.broadcast_to(jnp.pad(location, (0, 6))[:, None], (8, 128))
    a_t = jnp.swapaxes(a_store, 1, 2)
    half = inner_x.shape[1]
    cols = w_bc.shape[1]
    rate = jnp.broadcast_to(decay_rate[:, None], (heads, rows))
    hbm = pl.BlockSpec(memory_space=pl.ANY)
    vmem = pl.BlockSpec(memory_space=pltpu.VMEM)
    smem = pl.BlockSpec(memory_space=pltpu.SMEM)
    mixed, igrad, agrad, bgrad = pl.pallas_call(
        body,
        out_shape=(
            jax.ShapeDtypeStruct((rows, half), BF16),
            jax.ShapeDtypeStruct((rows, half), BF16),
            jax.ShapeDtypeStruct(a_t.shape, BF16),
            jax.ShapeDtypeStruct(b_store.shape, BF16),
        ),
        in_specs=[smem, hbm, hbm, vmem, vmem, hbm, hbm, hbm, hbm, vmem],
        out_specs=(hbm, hbm, hbm, hbm),
        scratch_shapes=[
            pltpu.VMEM((NZ, 1024, cols), BF16),
            pltpu.VMEM(tokens.shape, BF16),
            pltpu.VMEM((rows, half), BF16),
            pltpu.VMEM((rows, half), BF16),
            pltpu.VMEM(a_t.shape, BF16),
            pltpu.VMEM(b_store.shape, BF16),
            pltpu.VMEM((2, 8, 128), jnp.int32),
            pltpu.VMEM((2, NZ, 64, 640), BF16),
            pltpu.VMEM((NZ, 64, 640), BF16),
            pltpu.VMEM((NZ, 32, 640), BF16),
            pltpu.VMEM((NZ, 32, 640), BF16),
            pltpu.VMEM((32, 640), BF16),
            pltpu.VMEM((32, 640), BF16),
            pltpu.VMEM((2, NZ, 64, 640), BF16),
            pltpu.VMEM((64, half), BF16),
            pltpu.VMEM((64, cols), BF16),
            pltpu.VMEM((64, rows), F32),
            pltpu.VMEM((64, rows), F32),
            pltpu.VMEM((64, rows), BF16),
            pltpu.VMEM((heads, rows, rows), F32),
            pltpu.VMEM((heads, rows), F32),
            pltpu.VMEM((2, rows, rows), F32),
            pltpu.VMEM((rows, cols), F32),
            pltpu.VMEM((rows, cols), BF16),
            pltpu.VMEM((rows, cols), BF16),
            pltpu.VMEM((64, rows), F32),
            pltpu.VMEM((64, rows), F32),
            pltpu.VMEM((64, rows), BF16),
            pltpu.VMEM((4, rows, 1024), BF16),
            pltpu.VMEM((4, rows, 1024), BF16),
            pltpu.VMEM((rows, half), F32),
            pltpu.VMEM((rows, half), BF16),
            pltpu.VMEM((rows, half), BF16),
            pltpu.VMEM((2, NZ, 64, 640), BF16),
            pltpu.VMEM((NZ, 64, 640), BF16),
            pltpu.VMEM((NZ, 64, 640), BF16),
            pltpu.VMEM((64, 640), BF16),
            pltpu.VMEM((32, 640), BF16),
            pltpu.VMEM((32, 640), BF16),
            pltpu.VMEM((32, 640), BF16),
            pltpu.VMEM((2, NZ, 64, 640), BF16),
            pltpu.VMEM(a_t.shape, BF16),
            pltpu.VMEM(b_store.shape, BF16),
            pltpu.SemaphoreType.DMA((SLOTS,)),
            pltpu.SemaphoreType.DMA((SLOTS,)),
            pltpu.SemaphoreType.DMA((10,)),
        ],
        compiler_params=pltpu.CompilerParams(
            collective_id=0, has_side_effects=True, vmem_limit_bytes=56 * 1024 * 1024
        ),
    )(block_slot, tokens, inner_x, step_size.T, rate, grad_out, w_bc, a_t, b_store, loc)
    return mixed, igrad, jnp.swapaxes(agrad, 1, 2), bgrad


def solution(mesh):
    both = ("fsdp", "tenant")
    placed = (
        P(both, None),
        P(both, "tensor"),
        P(both, "tensor"),
        P("tensor"),
        P(both, "tensor"),
        P("fsdp", "tensor"),
        P(both, "tensor", None),
        P(both, None, "tensor"),
        P("tenant", None),
        P(both),
        P(),
    )
    return jax.shard_map(
        shards,
        mesh=mesh,
        in_specs=placed,
        out_specs=(
            P(both, "tensor"),
            P(both, "tensor"),
            P(both, "tensor", None),
            P(both, None, "tensor"),
        ),
        check_vma=False,
    )
```

```python
import jax
import jax.numpy as jnp
from jax import lax
from jax.experimental import pallas as pl
from jax.experimental.pallas import tpu as pltpu
from jax.sharding import PartitionSpec as P

MESH = pl.DeviceIdType.MESH
F32 = jnp.float32
BF16 = jnp.bfloat16
NZ = 8
HEADS_GRP = 32
NS = 256

X_, Z_, Y_, D_, XR = 0, 4, 36, 68, 84
LIST_, LOW, Q, PIN_ = 88, 90, 91, 92
CORE, ACROSS, Z1, Z2, OVER, GZ, GX, GC = 0, 1, 2, 5, 9, 10, 18, 26
FETCH, BACK = 96, 130
SLOTS = 164

NN = (((1,), (0,)), ((), ()))
NT = (((1,), (1,)), ((), ()))
TN = (((0,), (0,)), ((), ()))


def dot(a, b, dims=NN, precision=None):
    return lax.dot_general(a, b, dims, precision=precision, preferred_element_type=F32)


def body(
    slot_ref, list_ref, owner_ref, rate_ref, step_ref, tok_hbm, x_hbm, g_hbm, w_hbm, a_hbm, b_hbm,
    mixed_hbm, igrad_hbm, agrad_hbm, bgrad_hbm,
    w, tok, x, g, a_own, b_own, loc, listed, cand, rcore, rx, r1, r2, chunk, full,
    sel_a, sel_b, low_s, low_r, low_t, decay, tot, score_grad, acc, proj, gproj,
    q_s, q_r, q_t, psend, precv, part, mixed, igrad,
    bcand, brcore, br1, br2, bs, brx, bchunk, bfull, agrad, bgrad,
    ssem, rsem, lsem,
):
    f = lax.axis_index("fsdp")
    y = lax.axis_index("tenant")
    t = lax.axis_index("tensor")
    z = f // 4
    l = (f // 2) % 2
    c = f % 2
    p = y % 2
    rows = tok.shape[0]
    pairs = x.shape[1] // 128
    grp_pairs = pairs // 2

    def zat(d):
        return (z + d + NZ) % NZ

    def zdev(d):
        return (zat(d) * 4 + l * 2 + c, y, t)

    def ydev(d):
        return (f, (y + d + 4) % 4, t)

    sib = (z * 4 + l * 2 + (1 - c), y, t)
    xdev = (z * 4 + (1 - l) * 2 + c, y, t)
    tdev = (f, y, 1 - t)

    sent = []

    def send(src, dst, slot, dev):
        copy = pltpu.make_async_remote_copy(
            src_ref=src, dst_ref=dst, send_sem=ssem.at[slot], recv_sem=rsem.at[slot],
            device_id=dev, device_id_type=MESH,
        )
        copy.start()
        sent.append(copy)

    def got(dst, slot):
        pltpu.make_async_remote_copy(
            src_ref=dst, dst_ref=dst, send_sem=ssem.at[slot], recv_sem=rsem.at[slot],
            device_id=sib, device_id_type=MESH,
        ).wait_recv()

    def local(src, dst, slot):
        copy = pltpu.make_async_copy(src, dst, lsem.at[slot])
        copy.start()
        return copy

    def lside(which):
        return l if which == 0 else 1 - l

    def piece(d, which, par, h):
        first = pl.multiple_of((lside(which) * 2 + c) * 256 + par * 128 + h * 64, 64)
        return w.at[zat(d), pl.ds(first, 64), :]

    def move(part, slot, dev):
        send(part, part, slot, dev)

    def whole(d, which, core):
        first = pl.multiple_of((lside(which) * 2 + core) * 256, 256)
        return w.at[zat(d), pl.ds(first, 256), :]

    load_w = local(w_hbm, whole(0, 0, c), 0)
    load_a = local(a_hbm, a_own, 1)
    load_b = local(b_hbm, b_own, 2)
    load_x = local(x_hbm, x, 3)
    load_g = local(g_hbm, g, 4)
    load_tok = local(tok_hbm, tok, 5)

    barrier = pltpu.get_barrier_semaphore()
    partners = [sib, xdev, tdev] + [zdev(d) for d in range(1, NZ)] + [ydev(d) for d in range(1, 4)]
    for dev in partners:
        pl.semaphore_signal(barrier, inc=1, device_id=dev, device_id_type=MESH)
    pl.semaphore_wait(barrier, len(partners))

    loc[...] = jnp.where(
        lax.broadcasted_iota(jnp.int32, loc.shape, 0) == 0,
        owner_ref[list_ref[0, 0]],
        owner_ref[list_ref[0, 1]],
    )
    for j in range(2):
        send(loc, listed.at[j], LIST_ + j, ydev(2 - j))
    load_w.wait()
    for h in range(2):
        move(piece(0, 0, p, h), X_ + h, xdev)
        for way in range(2):
            move(piece(0, 0, p, h), Z_ + way * 16 + h, zdev(1 - 2 * way))
    send(whole(0, 0, c), whole(0, 0, c), D_, sib)

    upto = (
        lax.broadcasted_iota(jnp.int32, (rows, rows), 0)
        <= lax.broadcasted_iota(jnp.int32, (rows, rows), 1)
    ).astype(F32)
    tot[...] = dot(-step_ref[...], upto, precision=lax.Precision.HIGHEST)
    score_grad[...] = jnp.zeros_like(score_grad)
    acc[...] = jnp.zeros_like(acc)
    load_x.wait()
    load_g.wait()

    lanes = lax.broadcasted_iota(jnp.int32, (rows, 128), 1)

    def split_heads(values):
        wide = values.astype(F32)
        one = jnp.where(lanes < 64, wide, 0.0).astype(BF16)
        two = jnp.where(lanes >= 64, wide, 0.0).astype(BF16)
        return jnp.concatenate([one, two], axis=0)

    def decay_pairs(first, count):
        causal = lax.broadcasted_iota(jnp.int32, (rows, rows), 0) >= lax.broadcasted_iota(
            jnp.int32, (rows, rows), 1
        )

        def one_pair(k, carry):
            at = pl.multiple_of(k * 128, 128)
            both = split_heads(x[:, pl.ds(at, 128)])
            outer = dot(g[:, pl.ds(at, 128)], both, NT)
            total = jnp.zeros((rows, rows), F32)
            for i in range(2):
                head = 2 * k + i
                along = jnp.broadcast_to(tot[pl.ds(head, 1), :] * rate_ref[head], (rows, rows))
                spread = jnp.where(causal, along.T - along, -1e30)
                factor = jnp.exp(spread) * step_ref[pl.ds(head, 1), :]
                decay[head] = factor
                total += factor * outer[:, i * 128 : (i + 1) * 128]
            score_grad[k // grp_pairs] += total
            return carry

        lax.fori_loop(first, first + count, one_pair, 0)

    base = ((f * 4) + y) * 2
    for j in range(2):
        got(listed.at[j], LIST_ + j)

    def picked(j, k):
        return (listed[j, j : j + 1, :] == base + k).astype(F32)

    load_a.wait()
    load_b.wait()
    for j in range(2):
        m0, m1 = picked(j, 0), picked(j, 1)
        for zc in range(NZ):
            for i in range(5):
                src, at = (a_own, zc * 512 + i * 128) if i < 4 else (b_own, zc * 128)
                value = (
                    src[0, :, at : at + 128].astype(F32) * m0
                    + src[1, :, at : at + 128].astype(F32) * m1
                )
                cand[j, zc, :, i * 128 : (i + 1) * 128] = value.astype(BF16)
    send(cand.at[1 - c], rcore, FETCH + CORE, sib)
    mine = pl.ds(pl.multiple_of(32 * l, 32), 32)
    other = pl.ds(pl.multiple_of(32 * (1 - l), 32), 32)

    def reduce_start(own, one, two, at):
        send(own(3), one.at[0], at + Z1, zdev(1))
        send(own(4), one.at[1], at + Z1 + 1, zdev(2))
        send(own(-3), one.at[2], at + Z1 + 2, zdev(-1))
        send(own(1), two.at[0], at + Z2, zdev(1))
        send(own(-1), two.at[1], at + Z2 + 1, zdev(-1))

    def reduce_relay(own, one, two, at):
        for i in range(3):
            got(one.at[i], at + Z1 + i)
        up = one[0].astype(F32) + one[1].astype(F32) + own(2)[...].astype(F32)
        one[0] = up.astype(BF16)
        send(one.at[0], two.at[2], at + Z2 + 2, zdev(2))
        one[2] = (one[2].astype(F32) + own(-2)[...].astype(F32)).astype(BF16)
        send(one.at[2], two.at[3], at + Z2 + 3, zdev(-2))

    def reduce_end(own, two, at):
        total = own(0)[...].astype(F32)
        for i in range(4):
            got(two.at[i], at + Z2 + i)
            total += two[i].astype(F32)
        return total

    def held(buf, d, wide):
        return buf.at[c, zat(-d)] if wide else buf.at[c, zat(-d), mine, :]

    def gather_start(buf, at, wide):
        own = held(buf, 0, wide)
        for d in (2, -2, 1, -1):
            move(own, at + GZ + d % 8, zdev(d))
        move(own, at + (GC if wide else GX), sib if wide else xdev)

    def gather_in(buf, at, wide, d, hops=()):
        here = held(buf, d, wide)
        got(here, at + GZ + d % 8)
        for hop in hops:
            move(here, at + GZ + (d + hop) % 8, zdev(hop))
        move(here, at + (GC if wide else GX) + d % 8, sib if wide else xdev)

    def gather_core(buf, at, offs):
        for d in offs:
            got(buf.at[c, zat(-d), other, :], at + GX + d % 8)
            send(buf.at[c, zat(-d)], buf.at[c, zat(-d)], at + GC + d % 8, sib)

    def gather_end(buf, at):
        for d in range(NZ):
            got(buf.at[1 - c, zat(-d)], at + GC + d)


    def zstep(s, side):
        for h in range(2):
            for way, which, last in ((0, 0, 4), (1, 0, 2), (1, 1, 4), (0, 1, 2)):
                if s > last or which != side:
                    continue
                d = -s if way == 0 else s
                slot = Z_ + way * 16 + which * 8 + (s - 1) * 2 + h
                part_in = piece(d, which, p, h)
                got(part_in, slot)
                if s < last:
                    move(part_in, slot + 2, zdev(1 - 2 * way))
                move(part_in, Y_ + which * 16 + d % 8 * 2 + h, ydev(1 if which == 0 else -1))
                if s == 3:
                    move(part_in, XR + way * 2 + h, xdev)

    def xstep(way):
        d, which = (-3, 1) if way == 0 else (3, 0)
        for h in range(2):
            part_in = piece(d, which, p, h)
            got(part_in, XR + way * 2 + h)
            move(part_in, Y_ + which * 16 + d % 8 * 2 + h, ydev(1 if which == 0 else -1))

    def offsets(s):
        return (0,) if s == 0 else (4,) if s == 4 else (-s, s)

    def ystep(s):
        for d in offsets(s):
            for which in range(2):
                for h in range(2):
                    got(piece(d, which, 1 - p, h), Y_ + which * 16 + d % 8 * 2 + h)
                send(whole(d, which, c), whole(d, which, c), D_ + which * 8 + d % 8, sib)

    def forward(s):
        for d in offsets(s):
            for which in range(2):
                got(whole(d, which, 1 - c), D_ + which * 8 + d % 8)
        for d in offsets(s):
            at = zat(d)

            def part_n(n, carry, at=at):
                cols = pl.ds(pl.multiple_of(n * 256, 256), 256)
                acc[:, cols] += dot(
                    tok[:, pl.ds(pl.multiple_of(at * 1024, 1024), 1024)], w[at, :, cols]
                )
                return carry

            lax.fori_loop(0, 4, part_n, 0)

    quarter = pairs // 4

    def own_rows(k):
        return rx.at[zat(k)]

    for h in range(2):
        got(piece(0, 1, p, h), X_ + h)
        for way in range(2):
            move(piece(0, 1, p, h), Z_ + way * 16 + 8 + h, zdev(1 - 2 * way))
    got(rcore, FETCH + CORE)
    cand[c] = cand[c] + rcore[...]
    send(cand.at[c, :, other, :], rx, FETCH + ACROSS, xdev)
    zstep(1, 0)
    zstep(1, 1)
    decay_pairs(0, quarter * 2)
    got(rx, FETCH + ACROSS)
    rx[...] = rx[...] + cand[c, :, mine, :]
    reduce_start(own_rows, r1, r2, FETCH)
    zstep(2, 0)
    for h in range(2):
        move(piece(0, 0, 1 - p, h), X_ + 2 + h, xdev)
    decay_pairs(quarter * 2, quarter)
    ystep(1)
    zstep(2, 1)
    load_tok.wait()
    forward(1)
    reduce_relay(own_rows, r1, r2, FETCH)
    zstep(3, 0)
    zstep(3, 1)
    chunk[...] = reduce_end(own_rows, r2, FETCH).astype(BF16)
    send(chunk, full.at[c, z, mine, :], FETCH + OVER, ydev(2 + c))
    for h in range(2):
        got(piece(0, 1, 1 - p, h), X_ + 2 + h)
    send(whole(0, 1, c), whole(0, 1, c), D_ + 8, sib)
    ystep(2)
    decay_pairs(quarter * 3, quarter // 2)
    xstep(0)
    forward(0)
    got(full.at[c, z, mine, :], FETCH + OVER)
    gather_start(full, FETCH, False)
    zstep(4, 1)
    xstep(1)
    gather_in(full, FETCH, False, 2, (1, 2))
    gather_in(full, FETCH, False, -2, (-1,))
    zstep(4, 0)
    forward(2)
    ystep(3)
    for d in (1, -1, 3, -3, 4):
        gather_in(full, FETCH, False, d)
    decay_pairs(quarter * 3 + quarter // 2, quarter // 2)
    forward(3)
    gather_core(full, FETCH, (0, 2, -2, 1, -1, 3, -3, 4))
    ystep(4)
    gather_end(full, FETCH)
    slot = slot_ref[0]
    half = pl.multiple_of(t * 4096, 4096)
    low_part = jnp.zeros((64, rows), F32)
    for zc in range(NZ):
        piece_ab = full[slot, zc]
        sel_a[:, zc * 512 : (zc + 1) * 512] = piece_ab[:, :512]
        sel_b[:, zc * 128 : (zc + 1) * 128] = piece_ab[:, 512:]
        low_part += dot(piece_ab[:, :512], tok[:, pl.ds(half + zc * 512, 512)], NT)
    low_s[...] = low_part
    send(low_s, low_r, LOW, tdev)
    forward(4)
    got(low_r, LOW)
    low_t[...] = (low_s[...] + low_r[...]).astype(BF16)
    proj[...] = (acc[...] + dot(low_t[...], sel_b[...], TN)).astype(BF16)

    scores = []
    for gi in range(2):
        b_in = proj[:, gi * 512 : gi * 512 + 256]
        c_out = proj[:, gi * 512 + 256 : gi * 512 + 512]
        scores.append(dot(c_out, b_in, NT))
        sg = score_grad[gi].astype(BF16)
        gproj[:, gi * 512 : gi * 512 + 256] = dot(sg, c_out, TN).astype(BF16)
        gproj[:, gi * 512 + 256 : gi * 512 + 512] = dot(sg, b_in).astype(BF16)
    q_s[...] = dot(sel_b[...], gproj[...], NT)
    send(q_s, q_r, Q, tdev)
    for gi in range(2):
        score_grad[gi] = scores[gi]

    def back(at, n):
        return dot(gproj[...], w[at, pl.ds(pl.multiple_of(n * 256, 256), 256), :], NT)

    def partner(k):
        def partner_n(n, carry):
            cols = pl.ds(pl.multiple_of(n * 256, 256), 256)
            psend[k, :, cols] = back(4 * (1 - t) + k, n).astype(BF16)
            return carry

        lax.fori_loop(0, 4, partner_n, 0)

    def to_partner(k):
        send(psend.at[k], precv.at[k], PIN_ + k, tdev)

    partner(0)
    to_partner(0)

    got(q_r, Q)
    q_t[...] = (q_s[...] + q_r[...]).astype(BF16)
    for zc in range(NZ):
        ga = dot(q_t[...], tok[:, pl.ds(half + zc * 512, 512)])
        gb = dot(low_t[...], gproj[:, zc * 128 : (zc + 1) * 128])
        for j in range(2):
            chosen = jnp.where(slot == j, 1.0, 0.0).astype(F32)
            bcand[j, zc, :, :512] = (ga * chosen).astype(BF16)
            bcand[j, zc, :, 512:] = (gb * chosen).astype(BF16)
    send(bcand.at[1 - c], brcore, BACK + CORE, sib)
    partner(1)
    to_partner(1)

    def own_n(n, carry):
        cols = pl.ds(pl.multiple_of(n * 256, 256), 256)
        part[:, cols] = back(4 * t + n // 4, n % 4) + dot(q_t[...], sel_a[:, cols], TN)
        return carry

    def own_sum(k):
        return bcand.at[c, zat(k)]

    got(brcore, BACK + CORE)
    for zc in range(NZ):
        bcand[c, zc] = (bcand[c, zc].astype(F32) + brcore[zc].astype(F32)).astype(BF16)
    reduce_start(own_sum, br1, br2, BACK)
    partner(2)
    partner(3)
    lax.fori_loop(0, 5, own_n, 0)
    reduce_relay(own_sum, br1, br2, BACK)
    lax.fori_loop(5, 16, own_n, 0)

    def mix_pair(k, carry):
        at = pl.multiple_of(k * 128, 128)
        both = split_heads(x[:, pl.ds(at, 128)])
        score = score_grad[k // grp_pairs]
        weight = jnp.concatenate(
            [(decay[2 * k] * score).astype(BF16), (decay[2 * k + 1] * score).astype(BF16)], axis=1
        )
        mixed[:, pl.ds(at, 128)] = dot(weight, both).astype(BF16)
        return carry

    bs[...] = reduce_end(own_sum, br2, BACK).astype(BF16)
    send(bs.at[other, :], brx, BACK + ACROSS, xdev)
    got(brx, BACK + ACROSS)
    bchunk[...] = (bs[mine, :].astype(F32) + brx[...].astype(F32)).astype(BF16)
    send(bchunk, bfull.at[c, z, mine, :], BACK + OVER, ydev(2 - c))
    got(bfull.at[c, z, mine, :], BACK + OVER)
    move(held(bfull, 0, False), BACK + GX, xdev)
    for k in range(2, 4):
        to_partner(k)
    lax.fori_loop(0, pairs // 4, mix_pair, 0)
    got(bfull.at[c, z, other, :], BACK + GX)
    gather_start(bfull, BACK, True)
    lax.fori_loop(pairs // 4, pairs, mix_pair, 0)
    out_mixed = local(mixed, mixed_hbm, 6)
    gather_in(bfull, BACK, True, 2, (1, 2))
    gather_in(bfull, BACK, True, -2, (-1,))

    def total_k(k):
        got(precv.at[k], PIN_ + k)
        cols = slice(k * 1024, (k + 1) * 1024)
        igrad[:, cols] = (part[:, cols] + precv[k].astype(F32)).astype(BF16)

    total_k(0)
    total_k(1)
    for d in (1, -1, 3, -3, 4):
        gather_in(bfull, BACK, True, d)
    gather_end(bfull, BACK)
    for k in range(2):
        m0, m1 = picked(0, k), picked(1, k)
        for zc in range(NZ):
            for i in range(5):
                dst, at = (agrad, zc * 512 + i * 128) if i < 4 else (bgrad, zc * 128)
                lane = slice(i * 128, (i + 1) * 128)
                value = (
                    bfull[0, zc, :, lane].astype(F32) * m0 + bfull[1, zc, :, lane].astype(F32) * m1
                )
                dst[k, :, at : at + 128] = value.astype(BF16)
    out_a = local(agrad, agrad_hbm, 8)
    total_k(2)
    total_k(3)
    out_igrad = local(igrad, igrad_hbm, 7)
    out_b = local(bgrad, bgrad_hbm, 9)
    for copy in sent:
        copy.wait_send()
    for copy in (out_mixed, out_igrad, out_a, out_b):
        copy.wait()


def shards(
    tokens, inner_x, step_size, decay_rate, grad_out, w_bc,
    a_store, b_store, tenant_list, block_slot, owner_slot,
):
    rows = tokens.shape[0]
    heads = decay_rate.shape[0]
    a_t = jnp.swapaxes(a_store, 1, 2)
    half = inner_x.shape[1]
    cols = w_bc.shape[1]
    hbm = pl.BlockSpec(memory_space=pltpu.HBM)
    free = pl.BlockSpec(memory_space=pl.ANY)
    vmem = pl.BlockSpec(memory_space=pltpu.VMEM)
    smem = pl.BlockSpec(memory_space=pltpu.SMEM)
    mixed, igrad, agrad, bgrad = pl.pallas_call(
        body,
        out_shape=(
            jax.ShapeDtypeStruct((rows, half), BF16),
            jax.ShapeDtypeStruct((rows, half), BF16),
            jax.ShapeDtypeStruct(a_t.shape, BF16),
            jax.ShapeDtypeStruct(b_store.shape, BF16),
        ),
        in_specs=[smem, smem, smem, smem, vmem, hbm, hbm, hbm, hbm, hbm, hbm],
        out_specs=(free, free, free, free),
        scratch_shapes=[
            pltpu.VMEM((NZ, 1024, cols), BF16),
            pltpu.VMEM(tokens.shape, BF16),
            pltpu.VMEM((rows, half), BF16),
            pltpu.VMEM((rows, half), BF16),
            pltpu.VMEM(a_t.shape, BF16),
            pltpu.VMEM(b_store.shape, BF16),
            pltpu.VMEM((8, 128), jnp.int32),
            pltpu.VMEM((2, 8, 128), jnp.int32),
            pltpu.VMEM((2, NZ, 64, 640), BF16),
            pltpu.VMEM((NZ, 64, 640), BF16),
            pltpu.VMEM((NZ, 32, 640), BF16),
            pltpu.VMEM((3, 32, 640), BF16),
            pltpu.VMEM((4, 32, 640), BF16),
            pltpu.VMEM((32, 640), BF16),
            pltpu.VMEM((2, NZ, 64, 640), BF16),
            pltpu.VMEM((64, half), BF16),
            pltpu.VMEM((64, cols), BF16),
            pltpu.VMEM((64, rows), F32),
            pltpu.VMEM((64, rows), F32),
            pltpu.VMEM((64, rows), BF16),
            pltpu.VMEM((heads, rows, rows), F32),
            pltpu.VMEM((heads, rows), F32),
            pltpu.VMEM((2, rows, rows), F32),
            pltpu.VMEM((rows, cols), F32),
            pltpu.VMEM((rows, cols), BF16),
            pltpu.VMEM((rows, cols), BF16),
            pltpu.VMEM((64, rows), F32),
            pltpu.VMEM((64, rows), F32),
            pltpu.VMEM((64, rows), BF16),
            pltpu.VMEM((4, rows, 1024), BF16),
            pltpu.VMEM((4, rows, 1024), BF16),
            pltpu.VMEM((rows, half), F32),
            pltpu.VMEM((rows, half), BF16),
            pltpu.VMEM((rows, half), BF16),
            pltpu.VMEM((2, NZ, 64, 640), BF16),
            pltpu.VMEM((NZ, 64, 640), BF16),
            pltpu.VMEM((3, 64, 640), BF16),
            pltpu.VMEM((4, 64, 640), BF16),
            pltpu.VMEM((64, 640), BF16),
            pltpu.VMEM((32, 640), BF16),
            pltpu.VMEM((32, 640), BF16),
            pltpu.VMEM((2, NZ, 64, 640), BF16),
            pltpu.VMEM(a_t.shape, BF16),
            pltpu.VMEM(b_store.shape, BF16),
            pltpu.SemaphoreType.DMA((SLOTS,)),
            pltpu.SemaphoreType.DMA((SLOTS,)),
            pltpu.SemaphoreType.DMA((10,)),
        ],
        compiler_params=pltpu.CompilerParams(
            collective_id=0, has_side_effects=True, vmem_limit_bytes=56 * 1024 * 1024
        ),
    )(
        block_slot, tenant_list, owner_slot, decay_rate, step_size.T,
        tokens, inner_x, grad_out, w_bc, a_t, b_store,
    )
    return mixed, igrad, jnp.swapaxes(agrad, 1, 2), bgrad


def solution(mesh):
    both = ("fsdp", "tenant")
    placed = (
        P(both, None),
        P(both, "tensor"),
        P(both, "tensor"),
        P("tensor"),
        P(both, "tensor"),
        P("fsdp", "tensor"),
        P(both, "tensor", None),
        P(both, None, "tensor"),
        P("tenant", None),
        P(both),
        P(),
    )
    return jax.shard_map(
        shards,
        mesh=mesh,
        in_specs=placed,
        out_specs=(
            P(both, "tensor"),
            P(both, "tensor"),
            P(both, "tensor", None),
            P(both, None, "tensor"),
        ),
        check_vma=False,
    )
```

```python
import jax
import jax.numpy as jnp
from jax import lax
from jax.experimental import pallas as pl
from jax.experimental.pallas import tpu as pltpu
from jax.sharding import PartitionSpec as P

MESH = pl.DeviceIdType.MESH
F32 = jnp.float32
BF16 = jnp.bfloat16
NZ = 8
HEADS_GRP = 32
NS = 256

X_, Z_, Y_, D_, XR = 0, 4, 36, 68, 84
LIST_, LOW, Q, PIN_ = 88, 90, 91, 92
CORE, ACROSS, Z1, Z2, OVER, GZ, GX, GC = 0, 1, 2, 5, 9, 10, 18, 26
FETCH, BACK = 96, 130
SLOTS = 164

NN = (((1,), (0,)), ((), ()))
NT = (((1,), (1,)), ((), ()))
TN = (((0,), (0,)), ((), ()))


def dot(a, b, dims=NN, precision=None):
    return lax.dot_general(a, b, dims, precision=precision, preferred_element_type=F32)


def body(
    slot_ref, list_ref, owner_ref, rate_ref, step_ref, tok_hbm, x_hbm, g_hbm, w_hbm, a_hbm, b_hbm,
    mixed_hbm, igrad_hbm, agrad_hbm, bgrad_hbm,
    w, tok, x, g, a_own, b_own, loc, listed, cand, rcore, rx, r1, r2, chunk, full,
    sel_a, sel_b, low_s, low_r, low_t, decay, tot, score_grad, acc, proj, gproj,
    q_s, q_r, q_t, psend, precv, part, mixed, igrad,
    bcand, brcore, br1, br2, bs, brx, bchunk, bfull, agrad, bgrad,
    ssem, rsem, lsem,
):
    f = lax.axis_index("fsdp")
    y = lax.axis_index("tenant")
    t = lax.axis_index("tensor")
    z = f // 4
    l = (f // 2) % 2
    c = f % 2
    p = y % 2
    rows = tok.shape[0]
    pairs = x.shape[1] // 128
    grp_pairs = pairs // 2

    def zat(d):
        return (z + d + NZ) % NZ

    def zdev(d):
        return (zat(d) * 4 + l * 2 + c, y, t)

    def ydev(d):
        return (f, (y + d + 4) % 4, t)

    sib = (z * 4 + l * 2 + (1 - c), y, t)
    xdev = (z * 4 + (1 - l) * 2 + c, y, t)
    tdev = (f, y, 1 - t)

    sent = []

    def send(src, dst, slot, dev):
        copy = pltpu.make_async_remote_copy(
            src_ref=src, dst_ref=dst, send_sem=ssem.at[slot], recv_sem=rsem.at[slot],
            device_id=dev, device_id_type=MESH,
        )
        copy.start()
        sent.append(copy)

    def got(dst, slot):
        pltpu.make_async_remote_copy(
            src_ref=dst, dst_ref=dst, send_sem=ssem.at[slot], recv_sem=rsem.at[slot],
            device_id=sib, device_id_type=MESH,
        ).wait_recv()

    def local(src, dst, slot):
        copy = pltpu.make_async_copy(src, dst, lsem.at[slot])
        copy.start()
        return copy

    def lside(which):
        return l if which == 0 else 1 - l

    def piece(d, which, par, h):
        first = pl.multiple_of((lside(which) * 2 + c) * 256 + par * 128 + h * 64, 64)
        return w.at[zat(d), pl.ds(first, 64), :]

    def move(part, slot, dev):
        send(part, part, slot, dev)

    def whole(d, which, core):
        first = pl.multiple_of((lside(which) * 2 + core) * 256, 256)
        return w.at[zat(d), pl.ds(first, 256), :]

    load_w = local(w_hbm, whole(0, 0, c), 0)
    load_a = local(a_hbm, a_own, 1)
    load_b = local(b_hbm, b_own, 2)
    load_x = local(x_hbm, x, 3)
    load_g = local(g_hbm, g, 4)
    load_tok = local(tok_hbm, tok, 5)

    barrier = pltpu.get_barrier_semaphore()
    partners = [sib, xdev, tdev] + [zdev(d) for d in range(1, NZ)] + [ydev(d) for d in range(1, 4)]
    for dev in partners:
        pl.semaphore_signal(barrier, inc=1, device_id=dev, device_id_type=MESH)
    pl.semaphore_wait(barrier, len(partners))

    loc[...] = jnp.where(
        lax.broadcasted_iota(jnp.int32, loc.shape, 0) == 0,
        owner_ref[list_ref[0, 0]],
        owner_ref[list_ref[0, 1]],
    )
    for j in range(2):
        send(loc, listed.at[j], LIST_ + j, ydev(2 - j))
    load_w.wait()
    for h in range(2):
        move(piece(0, 0, p, h), X_ + h, xdev)
        for way in range(2):
            move(piece(0, 0, p, h), Z_ + way * 16 + h, zdev(1 - 2 * way))
    send(whole(0, 0, c), whole(0, 0, c), D_, sib)

    upto = (
        lax.broadcasted_iota(jnp.int32, (rows, rows), 0)
        <= lax.broadcasted_iota(jnp.int32, (rows, rows), 1)
    ).astype(F32)
    tot[...] = dot(-step_ref[...], upto, precision=lax.Precision.HIGHEST)
    score_grad[...] = jnp.zeros_like(score_grad)
    acc[...] = jnp.zeros_like(acc)
    load_x.wait()
    load_g.wait()

    lanes = lax.broadcasted_iota(jnp.int32, (rows, 128), 1)

    def split_heads(values):
        wide = values.astype(F32)
        one = jnp.where(lanes < 64, wide, 0.0).astype(BF16)
        two = jnp.where(lanes >= 64, wide, 0.0).astype(BF16)
        return jnp.concatenate([one, two], axis=0)

    def decay_pairs(first, count):
        causal = lax.broadcasted_iota(jnp.int32, (rows, rows), 0) >= lax.broadcasted_iota(
            jnp.int32, (rows, rows), 1
        )

        def one_pair(k, carry):
            at = pl.multiple_of(k * 128, 128)
            both = split_heads(x[:, pl.ds(at, 128)])
            outer = dot(g[:, pl.ds(at, 128)], both, NT)
            total = jnp.zeros((rows, rows), F32)
            for i in range(2):
                head = 2 * k + i
                along = jnp.broadcast_to(tot[pl.ds(head, 1), :] * rate_ref[head], (rows, rows))
                spread = jnp.where(causal, along.T - along, -1e30)
                factor = jnp.exp(spread) * step_ref[pl.ds(head, 1), :]
                decay[head] = factor
                total += factor * outer[:, i * 128 : (i + 1) * 128]
            score_grad[k // grp_pairs] += total
            return carry

        lax.fori_loop(first, first + count, one_pair, 0)

    base = ((f * 4) + y) * 2
    for j in range(2):
        got(listed.at[j], LIST_ + j)

    def picked(j, k):
        return (listed[j, j : j + 1, :] == base + k).astype(F32)

    load_a.wait()
    load_b.wait()
    for j in range(2):
        m0, m1 = picked(j, 0), picked(j, 1)
        for zc in range(NZ):
            for i in range(5):
                src, at = (a_own, zc * 512 + i * 128) if i < 4 else (b_own, zc * 128)
                value = (
                    src[0, :, at : at + 128].astype(F32) * m0
                    + src[1, :, at : at + 128].astype(F32) * m1
                )
                cand[j, zc, :, i * 128 : (i + 1) * 128] = value.astype(BF16)
    send(cand.at[1 - c], rcore, FETCH + CORE, sib)
    mine = pl.ds(pl.multiple_of(32 * l, 32), 32)
    other = pl.ds(pl.multiple_of(32 * (1 - l), 32), 32)

    turn = 1 - 2 * c

    def zturn(d):
        return zat(turn * d)

    def zway(d):
        return zdev(turn * d)

    def reduce_start(own, one, two, at):
        send(own(3), one.at[0], at + Z1, zway(1))
        send(own(4), one.at[1], at + Z1 + 1, zway(2))
        send(own(-3), one.at[2], at + Z1 + 2, zway(-1))
        send(own(1), two.at[0], at + Z2, zway(1))
        send(own(-1), two.at[1], at + Z2 + 1, zway(-1))

    def reduce_relay(own, one, two, at):
        for i in range(3):
            got(one.at[i], at + Z1 + i)
        up = one[0].astype(F32) + one[1].astype(F32) + own(2)[...].astype(F32)
        one[0] = up.astype(BF16)
        send(one.at[0], two.at[2], at + Z2 + 2, zway(2))
        one[2] = (one[2].astype(F32) + own(-2)[...].astype(F32)).astype(BF16)
        send(one.at[2], two.at[3], at + Z2 + 3, zway(-2))

    def reduce_end(own, two, at):
        total = own(0)[...].astype(F32)
        for i in range(4):
            got(two.at[i], at + Z2 + i)
            total += two[i].astype(F32)
        return total

    def held(buf, d, wide):
        return buf.at[c, zturn(-d)] if wide else buf.at[c, zturn(-d), mine, :]

    def gather_start(buf, at, wide):
        own = held(buf, 0, wide)
        for d in (2, -2, 1, -1):
            move(own, at + GZ + d % 8, zway(d))
        move(own, at + (GC if wide else GX), sib if wide else xdev)

    def gather_in(buf, at, wide, d, hops=()):
        here = held(buf, d, wide)
        got(here, at + GZ + d % 8)
        for hop in hops:
            move(here, at + GZ + (d + hop) % 8, zway(hop))
        move(here, at + (GC if wide else GX) + d % 8, sib if wide else xdev)

    def gather_core(buf, at, offs):
        for d in offs:
            got(buf.at[c, zturn(-d), other, :], at + GX + d % 8)
            send(buf.at[c, zturn(-d)], buf.at[c, zturn(-d)], at + GC + d % 8, sib)

    def gather_end(buf, at, offs):
        for d in offs:
            got(buf.at[1 - c, zturn(d)], at + GC + d % 8)


    def zstep(s, side):
        for h in range(2):
            for way, which, last in ((0, 0, 4), (1, 0, 2), (1, 1, 4), (0, 1, 2)):
                if s > last or which != side:
                    continue
                d = -s if way == 0 else s
                slot = Z_ + way * 16 + which * 8 + (s - 1) * 2 + h
                part_in = piece(d, which, p, h)
                got(part_in, slot)
                if s < last:
                    move(part_in, slot + 2, zdev(1 - 2 * way))
                move(part_in, Y_ + which * 16 + d % 8 * 2 + h, ydev(1 if which == 0 else -1))
                if s == 3:
                    move(part_in, XR + way * 2 + h, xdev)

    def xstep(way):
        d, which = (-3, 1) if way == 0 else (3, 0)
        for h in range(2):
            part_in = piece(d, which, p, h)
            got(part_in, XR + way * 2 + h)
            move(part_in, Y_ + which * 16 + d % 8 * 2 + h, ydev(1 if which == 0 else -1))

    def offsets(s):
        return (0,) if s == 0 else (4,) if s == 4 else (-s, s)

    def ystep(s):
        for d in offsets(s):
            for which in range(2):
                for h in range(2):
                    got(piece(d, which, 1 - p, h), Y_ + which * 16 + d % 8 * 2 + h)
                send(whole(d, which, c), whole(d, which, c), D_ + which * 8 + d % 8, sib)

    def forward(s):
        for d in offsets(s):
            for which in range(2):
                got(whole(d, which, 1 - c), D_ + which * 8 + d % 8)
        for d in offsets(s):
            at = zat(d)

            def part_n(n, carry, at=at):
                cols = pl.ds(pl.multiple_of(n * 256, 256), 256)
                acc[:, cols] += dot(
                    tok[:, pl.ds(pl.multiple_of(at * 1024, 1024), 1024)], w[at, :, cols]
                )
                return carry

            lax.fori_loop(0, 4, part_n, 0)

    quarter = pairs // 4

    def own_rows(k):
        return rx.at[zturn(k)]

    for h in range(2):
        got(piece(0, 1, p, h), X_ + h)
        for way in range(2):
            move(piece(0, 1, p, h), Z_ + way * 16 + 8 + h, zdev(1 - 2 * way))
    got(rcore, FETCH + CORE)
    cand[c] = cand[c] + rcore[...]
    send(cand.at[c, :, other, :], rx, FETCH + ACROSS, xdev)
    zstep(1, 0)
    zstep(1, 1)
    decay_pairs(0, quarter * 2)
    got(rx, FETCH + ACROSS)
    rx[...] = rx[...] + cand[c, :, mine, :]
    reduce_start(own_rows, r1, r2, FETCH)
    zstep(2, 0)
    for h in range(2):
        move(piece(0, 0, 1 - p, h), X_ + 2 + h, xdev)
    decay_pairs(quarter * 2, quarter)
    ystep(1)
    zstep(2, 1)
    load_tok.wait()
    forward(1)
    reduce_relay(own_rows, r1, r2, FETCH)
    zstep(3, 0)
    zstep(3, 1)
    chunk[...] = reduce_end(own_rows, r2, FETCH).astype(BF16)
    send(chunk, full.at[c, z, mine, :], FETCH + OVER, ydev(2 + c))
    for h in range(2):
        got(piece(0, 1, 1 - p, h), X_ + 2 + h)
    send(whole(0, 1, c), whole(0, 1, c), D_ + 8, sib)
    ystep(2)
    decay_pairs(quarter * 3, quarter // 2)
    xstep(0)
    forward(0)
    got(full.at[c, z, mine, :], FETCH + OVER)
    gather_start(full, FETCH, False)
    zstep(4, 1)
    xstep(1)
    gather_in(full, FETCH, False, 2, (1, 2))
    gather_in(full, FETCH, False, -2, (-1,))
    zstep(4, 0)
    forward(2)
    ystep(3)
    for d in (1, -1, 3, -3, 4):
        gather_in(full, FETCH, False, d)
    decay_pairs(quarter * 3 + quarter // 2, quarter // 2)
    forward(3)
    gather_core(full, FETCH, (0, 2, -2, 1, -1, 3, -3, 4))
    ystep(4)
    gather_end(full, FETCH, range(NZ))
    slot = slot_ref[0]
    half = pl.multiple_of(t * 4096, 4096)
    low_part = jnp.zeros((64, rows), F32)
    for zc in range(NZ):
        piece_ab = full[slot, zc]
        sel_a[:, zc * 512 : (zc + 1) * 512] = piece_ab[:, :512]
        sel_b[:, zc * 128 : (zc + 1) * 128] = piece_ab[:, 512:]
        low_part += dot(piece_ab[:, :512], tok[:, pl.ds(half + zc * 512, 512)], NT)
    low_s[...] = low_part
    send(low_s, low_r, LOW, tdev)
    forward(4)
    got(low_r, LOW)
    low_t[...] = (low_s[...] + low_r[...]).astype(BF16)
    proj[...] = (acc[...] + dot(low_t[...], sel_b[...], TN)).astype(BF16)

    scores = []
    for gi in range(2):
        b_in = proj[:, gi * 512 : gi * 512 + 256]
        c_out = proj[:, gi * 512 + 256 : gi * 512 + 512]
        scores.append(dot(c_out, b_in, NT))
        sg = score_grad[gi].astype(BF16)
        gproj[:, gi * 512 : gi * 512 + 256] = dot(sg, c_out, TN).astype(BF16)
        gproj[:, gi * 512 + 256 : gi * 512 + 512] = dot(sg, b_in).astype(BF16)
    q_s[...] = dot(sel_b[...], gproj[...], NT)
    send(q_s, q_r, Q, tdev)
    for gi in range(2):
        score_grad[gi] = scores[gi]

    def back(at, n):
        return dot(gproj[...], w[at, pl.ds(pl.multiple_of(n * 256, 256), 256), :], NT)

    def partner(k):
        def partner_n(n, carry):
            cols = pl.ds(pl.multiple_of(n * 256, 256), 256)
            psend[k, :, cols] = back(4 * (1 - t) + k, n).astype(BF16)
            return carry

        lax.fori_loop(0, 4, partner_n, 0)

    def to_partner(k):
        send(psend.at[k], precv.at[k], PIN_ + k, tdev)

    partner(0)
    to_partner(0)

    got(q_r, Q)
    q_t[...] = (q_s[...] + q_r[...]).astype(BF16)
    for zc in range(NZ):
        ga = dot(q_t[...], tok[:, pl.ds(half + zc * 512, 512)])
        gb = dot(low_t[...], gproj[:, zc * 128 : (zc + 1) * 128])
        for j in range(2):
            chosen = jnp.where(slot == j, 1.0, 0.0).astype(F32)
            bcand[j, zc, :, :512] = (ga * chosen).astype(BF16)
            bcand[j, zc, :, 512:] = (gb * chosen).astype(BF16)
    send(bcand.at[1 - c], brcore, BACK + CORE, sib)
    partner(1)
    to_partner(1)

    def own_n(n, carry):
        cols = pl.ds(pl.multiple_of(n * 256, 256), 256)
        part[:, cols] = back(4 * t + n // 4, n % 4) + dot(q_t[...], sel_a[:, cols], TN)
        return carry

    def own_sum(k):
        return bcand.at[c, zturn(k)]

    got(brcore, BACK + CORE)
    for zc in range(NZ):
        bcand[c, zc] = (bcand[c, zc].astype(F32) + brcore[zc].astype(F32)).astype(BF16)
    reduce_start(own_sum, br1, br2, BACK)
    partner(2)
    partner(3)
    lax.fori_loop(0, 5, own_n, 0)
    reduce_relay(own_sum, br1, br2, BACK)
    lax.fori_loop(5, 16, own_n, 0)

    def mix_pair(k, carry):
        at = pl.multiple_of(k * 128, 128)
        both = split_heads(x[:, pl.ds(at, 128)])
        score = score_grad[k // grp_pairs]
        weight = jnp.concatenate(
            [(decay[2 * k] * score).astype(BF16), (decay[2 * k + 1] * score).astype(BF16)], axis=1
        )
        mixed[:, pl.ds(at, 128)] = dot(weight, both).astype(BF16)
        return carry

    bs[...] = reduce_end(own_sum, br2, BACK).astype(BF16)
    send(bs.at[other, :], brx, BACK + ACROSS, xdev)
    got(brx, BACK + ACROSS)
    bchunk[...] = (bs[mine, :].astype(F32) + brx[...].astype(F32)).astype(BF16)
    send(bchunk, bfull.at[c, z, mine, :], BACK + OVER, ydev(2 - c))
    got(bfull.at[c, z, mine, :], BACK + OVER)
    move(held(bfull, 0, False), BACK + GX, xdev)
    for k in range(2, 4):
        to_partner(k)
    lax.fori_loop(0, pairs // 4, mix_pair, 0)
    got(bfull.at[c, z, other, :], BACK + GX)
    gather_start(bfull, BACK, True)
    lax.fori_loop(pairs // 4, pairs, mix_pair, 0)
    out_mixed = local(mixed, mixed_hbm, 6)
    gather_in(bfull, BACK, True, 2, (1, 2))
    gather_in(bfull, BACK, True, -2, (-1,))

    def total_k(k):
        got(precv.at[k], PIN_ + k)
        cols = slice(k * 1024, (k + 1) * 1024)
        igrad[:, cols] = (part[:, cols] + precv[k].astype(F32)).astype(BF16)

    total_k(0)
    total_k(1)
    masks = [[picked(j, k) for j in range(2)] for k in range(2)]

    def place(offs):
        for d in offs:
            at = zat(d)
            for k in range(2):
                for i in range(5):
                    dst, first = (agrad, at * 512 + i * 128) if i < 4 else (bgrad, at * 128)
                    lane = slice(i * 128, (i + 1) * 128)
                    value = (
                        bfull[0, at, :, lane].astype(F32) * masks[k][0]
                        + bfull[1, at, :, lane].astype(F32) * masks[k][1]
                    )
                    dst[k, :, pl.ds(pl.multiple_of(first, 128), 128)] = value.astype(BF16)

    for d in (1, -1):
        gather_in(bfull, BACK, True, d)
    gather_end(bfull, BACK, (0, 1, -1, 2, -2))
    place((0, 1, -1, 2, -2))
    for d in (3, -3, 4):
        gather_in(bfull, BACK, True, d)
    gather_end(bfull, BACK, (3, -3, 4))
    place((3, -3, 4))
    out_a = local(agrad, agrad_hbm, 8)
    total_k(2)
    total_k(3)
    out_igrad = local(igrad, igrad_hbm, 7)
    out_b = local(bgrad, bgrad_hbm, 9)
    for copy in sent:
        copy.wait_send()
    for copy in (out_mixed, out_igrad, out_a, out_b):
        copy.wait()


def shards(
    tokens, inner_x, step_size, decay_rate, grad_out, w_bc,
    a_store, b_store, tenant_list, block_slot, owner_slot,
):
    rows = tokens.shape[0]
    heads = decay_rate.shape[0]
    a_t = jnp.swapaxes(a_store, 1, 2)
    half = inner_x.shape[1]
    cols = w_bc.shape[1]
    hbm = pl.BlockSpec(memory_space=pltpu.HBM)
    free = pl.BlockSpec(memory_space=pl.ANY)
    vmem = pl.BlockSpec(memory_space=pltpu.VMEM)
    smem = pl.BlockSpec(memory_space=pltpu.SMEM)
    mixed, igrad, agrad, bgrad = pl.pallas_call(
        body,
        out_shape=(
            jax.ShapeDtypeStruct((rows, half), BF16),
            jax.ShapeDtypeStruct((rows, half), BF16),
            jax.ShapeDtypeStruct(a_t.shape, BF16),
            jax.ShapeDtypeStruct(b_store.shape, BF16),
        ),
        in_specs=[smem, smem, smem, smem, vmem, hbm, hbm, hbm, hbm, hbm, hbm],
        out_specs=(free, free, free, free),
        scratch_shapes=[
            pltpu.VMEM((NZ, 1024, cols), BF16),
            pltpu.VMEM(tokens.shape, BF16),
            pltpu.VMEM((rows, half), BF16),
            pltpu.VMEM((rows, half), BF16),
            pltpu.VMEM(a_t.shape, BF16),
            pltpu.VMEM(b_store.shape, BF16),
            pltpu.VMEM((8, 128), jnp.int32),
            pltpu.VMEM((2, 8, 128), jnp.int32),
            pltpu.VMEM((2, NZ, 64, 640), BF16),
            pltpu.VMEM((NZ, 64, 640), BF16),
            pltpu.VMEM((NZ, 32, 640), BF16),
            pltpu.VMEM((3, 32, 640), BF16),
            pltpu.VMEM((4, 32, 640), BF16),
            pltpu.VMEM((32, 640), BF16),
            pltpu.VMEM((2, NZ, 64, 640), BF16),
            pltpu.VMEM((64, half), BF16),
            pltpu.VMEM((64, cols), BF16),
            pltpu.VMEM((64, rows), F32),
            pltpu.VMEM((64, rows), F32),
            pltpu.VMEM((64, rows), BF16),
            pltpu.VMEM((heads, rows, rows), F32),
            pltpu.VMEM((heads, rows), F32),
            pltpu.VMEM((2, rows, rows), F32),
            pltpu.VMEM((rows, cols), F32),
            pltpu.VMEM((rows, cols), BF16),
            pltpu.VMEM((rows, cols), BF16),
            pltpu.VMEM((64, rows), F32),
            pltpu.VMEM((64, rows), F32),
            pltpu.VMEM((64, rows), BF16),
            pltpu.VMEM((4, rows, 1024), BF16),
            pltpu.VMEM((4, rows, 1024), BF16),
            pltpu.VMEM((rows, half), F32),
            pltpu.VMEM((rows, half), BF16),
            pltpu.VMEM((rows, half), BF16),
            pltpu.VMEM((2, NZ, 64, 640), BF16),
            pltpu.VMEM((NZ, 64, 640), BF16),
            pltpu.VMEM((3, 64, 640), BF16),
            pltpu.VMEM((4, 64, 640), BF16),
            pltpu.VMEM((64, 640), BF16),
            pltpu.VMEM((32, 640), BF16),
            pltpu.VMEM((32, 640), BF16),
            pltpu.VMEM((2, NZ, 64, 640), BF16),
            pltpu.VMEM(a_t.shape, BF16),
            pltpu.VMEM(b_store.shape, BF16),
            pltpu.SemaphoreType.DMA((SLOTS,)),
            pltpu.SemaphoreType.DMA((SLOTS,)),
            pltpu.SemaphoreType.DMA((10,)),
        ],
        compiler_params=pltpu.CompilerParams(
            collective_id=0, has_side_effects=True, vmem_limit_bytes=56 * 1024 * 1024
        ),
    )(
        block_slot, tenant_list, owner_slot, decay_rate, step_size.T,
        tokens, inner_x, grad_out, w_bc, a_t, b_store,
    )
    return mixed, igrad, jnp.swapaxes(agrad, 1, 2), bgrad


def solution(mesh):
    both = ("fsdp", "tenant")
    placed = (
        P(both, None),
        P(both, "tensor"),
        P(both, "tensor"),
        P("tensor"),
        P(both, "tensor"),
        P("fsdp", "tensor"),
        P(both, "tensor", None),
        P(both, None, "tensor"),
        P("tenant", None),
        P(both),
        P(),
    )
    return jax.shard_map(
        shards,
        mesh=mesh,
        in_specs=placed,
        out_specs=(
            P(both, "tensor"),
            P(both, "tensor"),
            P(both, "tensor", None),
            P(both, None, "tensor"),
        ),
        check_vma=False,
    )
```

```python
import jax
import jax.numpy as jnp
from jax import lax
from jax.experimental import pallas as pl
from jax.experimental.pallas import tpu as pltpu
from jax.sharding import PartitionSpec as P

MESH = pl.DeviceIdType.MESH
F32 = jnp.float32
BF16 = jnp.bfloat16
NZ = 8
HEADS_GRP = 32
NS = 256

X_, Z_, Y_, D_, XR = 0, 4, 36, 68, 84
LIST_, LOW, Q, PIN_ = 88, 90, 91, 92
CORE, ACROSS, Z1, Z2, OVER, GZ, GX, GC = 0, 1, 2, 5, 9, 10, 18, 26
FETCH, BACK = 96, 130
SLOTS = 164

NN = (((1,), (0,)), ((), ()))
NT = (((1,), (1,)), ((), ()))
TN = (((0,), (0,)), ((), ()))


def dot(a, b, dims=NN, precision=None):
    return lax.dot_general(a, b, dims, precision=precision, preferred_element_type=F32)


def body(
    slot_ref, list_ref, owner_ref, rate_ref, step_ref, tok_hbm, x_hbm, g_hbm, w_hbm, a_hbm, b_hbm,
    mixed_hbm, igrad_hbm, agrad_hbm, bgrad_hbm,
    w, tok, x, g, a_own, b_own, loc, listed, cand, rcore, rx, r1, r2, chunk, full,
    sel_a, sel_b, low_s, low_r, low_t, decay, tot, score_grad, acc, proj, gproj,
    q_s, q_r, q_t, psend, precv, part, mixed, igrad,
    bcand, brcore, br1, br2, bs, brx, bchunk, bfull, agrad, bgrad,
    ssem, rsem, lsem,
):
    f = lax.axis_index("fsdp")
    y = lax.axis_index("tenant")
    t = lax.axis_index("tensor")
    z = f // 4
    l = (f // 2) % 2
    c = f % 2
    p = y % 2
    rows = tok.shape[0]
    pairs = x.shape[1] // 128
    grp_pairs = pairs // 2

    def zat(d):
        return (z + d + NZ) % NZ

    def zdev(d):
        return (zat(d) * 4 + l * 2 + c, y, t)

    def ydev(d):
        return (f, (y + d + 4) % 4, t)

    sib = (z * 4 + l * 2 + (1 - c), y, t)
    xdev = (z * 4 + (1 - l) * 2 + c, y, t)
    tdev = (f, y, 1 - t)

    sent = []

    def send(src, dst, slot, dev):
        copy = pltpu.make_async_remote_copy(
            src_ref=src, dst_ref=dst, send_sem=ssem.at[slot], recv_sem=rsem.at[slot],
            device_id=dev, device_id_type=MESH,
        )
        copy.start()
        sent.append(copy)

    def got(dst, slot):
        pltpu.make_async_remote_copy(
            src_ref=dst, dst_ref=dst, send_sem=ssem.at[slot], recv_sem=rsem.at[slot],
            device_id=sib, device_id_type=MESH,
        ).wait_recv()

    def local(src, dst, slot):
        copy = pltpu.make_async_copy(src, dst, lsem.at[slot])
        copy.start()
        return copy

    def lside(which):
        return l if which == 0 else 1 - l

    def piece(d, which, par, h):
        first = pl.multiple_of((lside(which) * 2 + c) * 256 + par * 128 + h * 64, 64)
        return w.at[zat(d), pl.ds(first, 64), :]

    def move(part, slot, dev):
        send(part, part, slot, dev)

    def whole(d, which, core):
        first = pl.multiple_of((lside(which) * 2 + core) * 256, 256)
        return w.at[zat(d), pl.ds(first, 256), :]

    load_w = local(w_hbm, whole(0, 0, c), 0)
    load_a = local(a_hbm, a_own, 1)
    load_b = local(b_hbm, b_own, 2)
    load_x = local(x_hbm, x, 3)
    load_g = local(g_hbm, g, 4)
    load_tok = local(tok_hbm, tok, 5)

    barrier = pltpu.get_barrier_semaphore()
    partners = [sib, xdev, tdev] + [zdev(d) for d in range(1, NZ)] + [ydev(d) for d in range(1, 4)]
    for dev in partners:
        pl.semaphore_signal(barrier, inc=1, device_id=dev, device_id_type=MESH)
    pl.semaphore_wait(barrier, len(partners))

    loc[...] = jnp.where(
        lax.broadcasted_iota(jnp.int32, loc.shape, 0) == 0,
        owner_ref[list_ref[0, 0]],
        owner_ref[list_ref[0, 1]],
    )
    for j in range(2):
        send(loc, listed.at[j], LIST_ + j, ydev(2 - j))
    load_w.wait()
    for h in range(2):
        move(piece(0, 0, p, h), X_ + h, xdev)
        for way in range(2):
            move(piece(0, 0, p, h), Z_ + way * 16 + h, zdev(1 - 2 * way))
    send(whole(0, 0, c), whole(0, 0, c), D_, sib)

    upto = (
        lax.broadcasted_iota(jnp.int32, (rows, rows), 0)
        <= lax.broadcasted_iota(jnp.int32, (rows, rows), 1)
    ).astype(F32)
    tot[...] = dot(-step_ref[...], upto, precision=lax.Precision.HIGHEST)
    score_grad[...] = jnp.zeros_like(score_grad)
    acc[...] = jnp.zeros_like(acc)
    load_x.wait()
    load_g.wait()

    lanes = lax.broadcasted_iota(jnp.int32, (rows, 128), 1)

    def split_heads(values):
        wide = values.astype(F32)
        one = jnp.where(lanes < 64, wide, 0.0).astype(BF16)
        two = jnp.where(lanes >= 64, wide, 0.0).astype(BF16)
        return jnp.concatenate([one, two], axis=0)

    def decay_pairs(first, count):
        causal = lax.broadcasted_iota(jnp.int32, (rows, rows), 0) >= lax.broadcasted_iota(
            jnp.int32, (rows, rows), 1
        )

        def one_pair(k, carry):
            at = pl.multiple_of(k * 128, 128)
            both = split_heads(x[:, pl.ds(at, 128)])
            outer = dot(g[:, pl.ds(at, 128)], both, NT)
            total = jnp.zeros((rows, rows), F32)
            for i in range(2):
                head = 2 * k + i
                along = jnp.broadcast_to(tot[pl.ds(head, 1), :] * rate_ref[head], (rows, rows))
                spread = jnp.where(causal, along.T - along, -1e30)
                factor = jnp.exp(spread) * step_ref[pl.ds(head, 1), :]
                decay[head] = factor
                total += factor * outer[:, i * 128 : (i + 1) * 128]
            score_grad[k // grp_pairs] += total
            return carry

        lax.fori_loop(first, first + count, one_pair, 0)

    base = ((f * 4) + y) * 2
    for j in range(2):
        got(listed.at[j], LIST_ + j)

    def picked(j, k):
        return (listed[j, j : j + 1, :] == base + k).astype(F32)

    load_a.wait()
    load_b.wait()
    for j in range(2):
        m0, m1 = picked(j, 0), picked(j, 1)
        for zc in range(NZ):
            for i in range(5):
                src, at = (a_own, zc * 512 + i * 128) if i < 4 else (b_own, zc * 128)
                value = (
                    src[0, :, at : at + 128].astype(F32) * m0
                    + src[1, :, at : at + 128].astype(F32) * m1
                )
                cand[j, zc, :, i * 128 : (i + 1) * 128] = value.astype(BF16)
    send(cand.at[1 - c], rcore, FETCH + CORE, sib)
    mine = pl.ds(pl.multiple_of(32 * l, 32), 32)
    other = pl.ds(pl.multiple_of(32 * (1 - l), 32), 32)

    turn = 1 - 2 * c

    def zturn(d):
        return zat(turn * d)

    def zway(d):
        return zdev(turn * d)

    def reduce_start(own, one, two, at):
        send(own(3), one.at[0], at + Z1, zway(1))
        send(own(4), one.at[1], at + Z1 + 1, zway(2))
        send(own(-3), one.at[2], at + Z1 + 2, zway(-1))
        send(own(1), two.at[0], at + Z2, zway(1))
        send(own(-1), two.at[1], at + Z2 + 1, zway(-1))

    def reduce_relay(own, one, two, at):
        for i in range(3):
            got(one.at[i], at + Z1 + i)
        up = one[0].astype(F32) + one[1].astype(F32) + own(2)[...].astype(F32)
        one[0] = up.astype(BF16)
        send(one.at[0], two.at[2], at + Z2 + 2, zway(2))
        one[2] = (one[2].astype(F32) + own(-2)[...].astype(F32)).astype(BF16)
        send(one.at[2], two.at[3], at + Z2 + 3, zway(-2))

    def reduce_end(own, two, at):
        total = own(0)[...].astype(F32)
        for i in range(4):
            got(two.at[i], at + Z2 + i)
            total += two[i].astype(F32)
        return total

    def held(buf, d, wide):
        return buf.at[c, zturn(-d)] if wide else buf.at[c, zturn(-d), mine, :]

    def gather_start(buf, at, wide):
        own = held(buf, 0, wide)
        for d in (2, -2, 1, -1):
            move(own, at + GZ + d % 8, zway(d))
        move(own, at + (GC if wide else GX), sib if wide else xdev)

    def gather_in(buf, at, wide, d, hops=()):
        here = held(buf, d, wide)
        got(here, at + GZ + d % 8)
        for hop in hops:
            move(here, at + GZ + (d + hop) % 8, zway(hop))
        move(here, at + (GC if wide else GX) + d % 8, sib if wide else xdev)

    def gather_core(buf, at, offs):
        for d in offs:
            got(buf.at[c, zturn(-d), other, :], at + GX + d % 8)
            send(buf.at[c, zturn(-d)], buf.at[c, zturn(-d)], at + GC + d % 8, sib)

    def gather_end(buf, at, offs):
        for d in offs:
            got(buf.at[1 - c, zturn(d)], at + GC + d % 8)


    def zstep(s, side):
        for h in range(2):
            for way, which, last in ((0, 0, 4), (1, 0, 2), (1, 1, 4), (0, 1, 2)):
                if s > last or which != side:
                    continue
                d = -s if way == 0 else s
                slot = Z_ + way * 16 + which * 8 + (s - 1) * 2 + h
                part_in = piece(d, which, p, h)
                got(part_in, slot)
                if s < last:
                    move(part_in, slot + 2, zdev(1 - 2 * way))
                move(part_in, Y_ + which * 16 + d % 8 * 2 + h, ydev(1 if which == 0 else -1))
                if s == 3:
                    move(part_in, XR + way * 2 + h, xdev)

    def xstep(way):
        d, which = (-3, 1) if way == 0 else (3, 0)
        for h in range(2):
            part_in = piece(d, which, p, h)
            got(part_in, XR + way * 2 + h)
            move(part_in, Y_ + which * 16 + d % 8 * 2 + h, ydev(1 if which == 0 else -1))

    def offsets(s):
        return (0,) if s == 0 else (4,) if s == 4 else (-s, s)

    def ystep(s):
        for d in offsets(s):
            for which in range(2):
                for h in range(2):
                    got(piece(d, which, 1 - p, h), Y_ + which * 16 + d % 8 * 2 + h)
                send(whole(d, which, c), whole(d, which, c), D_ + which * 8 + d % 8, sib)

    def forward(s):
        for d in offsets(s):
            for which in range(2):
                got(whole(d, which, 1 - c), D_ + which * 8 + d % 8)
        for d in offsets(s):
            at = zat(d)

            def part_n(n, carry, at=at):
                cols = pl.ds(pl.multiple_of(n * 256, 256), 256)
                acc[:, cols] += dot(
                    tok[:, pl.ds(pl.multiple_of(at * 1024, 1024), 1024)], w[at, :, cols]
                )
                return carry

            lax.fori_loop(0, 4, part_n, 0)

    quarter = pairs // 4

    def own_rows(k):
        return rx.at[zturn(k)]

    for h in range(2):
        got(piece(0, 1, p, h), X_ + h)
        for way in range(2):
            move(piece(0, 1, p, h), Z_ + way * 16 + 8 + h, zdev(1 - 2 * way))
    got(rcore, FETCH + CORE)
    cand[c] = cand[c] + rcore[...]
    send(cand.at[c, :, other, :], rx, FETCH + ACROSS, xdev)
    zstep(1, 0)
    zstep(1, 1)
    decay_pairs(0, quarter * 2)
    got(rx, FETCH + ACROSS)
    rx[...] = rx[...] + cand[c, :, mine, :]
    reduce_start(own_rows, r1, r2, FETCH)
    zstep(2, 0)
    for h in range(2):
        move(piece(0, 0, 1 - p, h), X_ + 2 + h, xdev)
    decay_pairs(quarter * 2, quarter)
    ystep(1)
    zstep(2, 1)
    load_tok.wait()
    forward(1)
    reduce_relay(own_rows, r1, r2, FETCH)
    zstep(3, 0)
    zstep(3, 1)
    chunk[...] = reduce_end(own_rows, r2, FETCH).astype(BF16)
    send(chunk, full.at[c, z, mine, :], FETCH + OVER, ydev(2 + c))
    for h in range(2):
        got(piece(0, 1, 1 - p, h), X_ + 2 + h)
    send(whole(0, 1, c), whole(0, 1, c), D_ + 8, sib)
    ystep(2)
    decay_pairs(quarter * 3, quarter // 2)
    xstep(0)
    forward(0)
    got(full.at[c, z, mine, :], FETCH + OVER)
    gather_start(full, FETCH, False)
    zstep(4, 1)
    xstep(1)
    gather_in(full, FETCH, False, 2, (1, 2))
    gather_in(full, FETCH, False, -2, (-1,))
    zstep(4, 0)
    forward(2)
    ystep(3)
    for d in (1, -1, 3, -3, 4):
        gather_in(full, FETCH, False, d)
    decay_pairs(quarter * 3 + quarter // 2, quarter // 2)
    forward(3)
    gather_core(full, FETCH, (0, 2, -2, 1, -1, 3, -3, 4))
    ystep(4)
    gather_end(full, FETCH, range(NZ))
    slot = slot_ref[0]
    half = pl.multiple_of(t * 4096, 4096)
    low_part = jnp.zeros((64, rows), F32)
    for zc in range(NZ):
        piece_ab = full[slot, zc]
        sel_a[:, zc * 512 : (zc + 1) * 512] = piece_ab[:, :512]
        sel_b[:, zc * 128 : (zc + 1) * 128] = piece_ab[:, 512:]
        low_part += dot(piece_ab[:, :512], tok[:, pl.ds(half + zc * 512, 512)], NT)
    low_s[...] = low_part
    send(low_s, low_r, LOW, tdev)
    forward(4)
    got(low_r, LOW)
    low_t[...] = (low_s[...] + low_r[...]).astype(BF16)
    proj[...] = (acc[...] + dot(low_t[...], sel_b[...], TN)).astype(BF16)

    for gi in range(2):
        b_in = proj[:, gi * 512 : gi * 512 + 256]
        c_out = proj[:, gi * 512 + 256 : gi * 512 + 512]
        sg = score_grad[gi].astype(BF16)
        gproj[:, gi * 512 : gi * 512 + 256] = dot(sg, c_out, TN).astype(BF16)
        gproj[:, gi * 512 + 256 : gi * 512 + 512] = dot(sg, b_in).astype(BF16)
    q_s[...] = dot(sel_b[...], gproj[...], NT)
    send(q_s, q_r, Q, tdev)
    for gi in range(2):
        c_out = proj[:, gi * 512 + 256 : gi * 512 + 512]
        score_grad[gi] = dot(c_out, proj[:, gi * 512 : gi * 512 + 256], NT)

    def back(at, n):
        return dot(gproj[...], w[at, pl.ds(pl.multiple_of(n * 256, 256), 256), :], NT)

    def partner(k):
        def partner_n(n, carry):
            cols = pl.ds(pl.multiple_of(n * 256, 256), 256)
            psend[k, :, cols] = back(4 * (1 - t) + k, n).astype(BF16)
            return carry

        lax.fori_loop(0, 4, partner_n, 0)

    def to_partner(k):
        send(psend.at[k], precv.at[k], PIN_ + k, tdev)

    partner(0)
    to_partner(0)

    got(q_r, Q)
    q_t[...] = (q_s[...] + q_r[...]).astype(BF16)
    for zc in range(NZ):
        ga = dot(q_t[...], tok[:, pl.ds(half + zc * 512, 512)])
        gb = dot(low_t[...], gproj[:, zc * 128 : (zc + 1) * 128])
        for j in range(2):
            chosen = jnp.where(slot == j, 1.0, 0.0).astype(F32)
            bcand[j, zc, :, :512] = (ga * chosen).astype(BF16)
            bcand[j, zc, :, 512:] = (gb * chosen).astype(BF16)
    send(bcand.at[1 - c], brcore, BACK + CORE, sib)
    partner(1)
    to_partner(1)

    def own_n(n, carry):
        cols = pl.ds(pl.multiple_of(n * 256, 256), 256)
        part[:, cols] = back(4 * t + n // 4, n % 4) + dot(q_t[...], sel_a[:, cols], TN)
        return carry

    def own_sum(k):
        return bcand.at[c, zturn(k)]

    got(brcore, BACK + CORE)
    for zc in range(NZ):
        bcand[c, zc] = (bcand[c, zc].astype(F32) + brcore[zc].astype(F32)).astype(BF16)
    reduce_start(own_sum, br1, br2, BACK)
    partner(2)
    to_partner(2)
    partner(3)
    lax.fori_loop(0, 5, own_n, 0)
    reduce_relay(own_sum, br1, br2, BACK)
    lax.fori_loop(5, 16, own_n, 0)

    def mix_pair(k, carry):
        at = pl.multiple_of(k * 128, 128)
        both = split_heads(x[:, pl.ds(at, 128)])
        score = score_grad[k // grp_pairs]
        weight = jnp.concatenate(
            [(decay[2 * k] * score).astype(BF16), (decay[2 * k + 1] * score).astype(BF16)], axis=1
        )
        mixed[:, pl.ds(at, 128)] = dot(weight, both).astype(BF16)
        return carry

    bs[...] = reduce_end(own_sum, br2, BACK).astype(BF16)
    send(bs.at[other, :], brx, BACK + ACROSS, xdev)
    got(brx, BACK + ACROSS)
    bchunk[...] = (bs[mine, :].astype(F32) + brx[...].astype(F32)).astype(BF16)
    send(bchunk, bfull.at[c, z, mine, :], BACK + OVER, ydev(2 - c))
    got(bfull.at[c, z, mine, :], BACK + OVER)
    move(held(bfull, 0, False), BACK + GX, xdev)
    to_partner(3)
    lax.fori_loop(0, pairs // 4, mix_pair, 0)
    got(bfull.at[c, z, other, :], BACK + GX)
    gather_start(bfull, BACK, True)
    lax.fori_loop(pairs // 4, pairs, mix_pair, 0)
    out_mixed = local(mixed, mixed_hbm, 6)
    gather_in(bfull, BACK, True, 2, (1, 2))
    gather_in(bfull, BACK, True, -2, (-1,))

    def total_k(k):
        got(precv.at[k], PIN_ + k)
        cols = slice(k * 1024, (k + 1) * 1024)
        igrad[:, cols] = (part[:, cols] + precv[k].astype(F32)).astype(BF16)

    total_k(0)
    total_k(1)
    masks = [[picked(j, k) for j in range(2)] for k in range(2)]

    def place(offs):
        for d in offs:
            at = zat(d)
            for k in range(2):
                for i in range(5):
                    dst, first = (agrad, at * 512 + i * 128) if i < 4 else (bgrad, at * 128)
                    lane = slice(i * 128, (i + 1) * 128)
                    value = (
                        bfull[0, at, :, lane].astype(F32) * masks[k][0]
                        + bfull[1, at, :, lane].astype(F32) * masks[k][1]
                    )
                    dst[k, :, pl.ds(pl.multiple_of(first, 128), 128)] = value.astype(BF16)

    for d in (1, -1):
        gather_in(bfull, BACK, True, d)
    gather_end(bfull, BACK, (0, 1, -1, 2, -2))
    place((0, 1, -1, 2, -2))
    total_k(2)
    for d in (3, -3, 4):
        gather_in(bfull, BACK, True, d)
    gather_end(bfull, BACK, (3, -3, 4))
    place((3, -3, 4))
    out_a = local(agrad, agrad_hbm, 8)
    total_k(3)
    out_igrad = local(igrad, igrad_hbm, 7)
    out_b = local(bgrad, bgrad_hbm, 9)
    for copy in sent:
        copy.wait_send()
    for copy in (out_mixed, out_igrad, out_a, out_b):
        copy.wait()


def shards(
    tokens, inner_x, step_size, decay_rate, grad_out, w_bc,
    a_store, b_store, tenant_list, block_slot, owner_slot,
):
    rows = tokens.shape[0]
    heads = decay_rate.shape[0]
    a_t = jnp.swapaxes(a_store, 1, 2)
    half = inner_x.shape[1]
    cols = w_bc.shape[1]
    hbm = pl.BlockSpec(memory_space=pltpu.HBM)
    free = pl.BlockSpec(memory_space=pl.ANY)
    vmem = pl.BlockSpec(memory_space=pltpu.VMEM)
    smem = pl.BlockSpec(memory_space=pltpu.SMEM)
    mixed, igrad, agrad, bgrad = pl.pallas_call(
        body,
        out_shape=(
            jax.ShapeDtypeStruct((rows, half), BF16),
            jax.ShapeDtypeStruct((rows, half), BF16),
            jax.ShapeDtypeStruct(a_t.shape, BF16),
            jax.ShapeDtypeStruct(b_store.shape, BF16),
        ),
        in_specs=[smem, smem, smem, smem, vmem, hbm, hbm, hbm, hbm, hbm, hbm],
        out_specs=(free, free, free, free),
        scratch_shapes=[
            pltpu.VMEM((NZ, 1024, cols), BF16),
            pltpu.VMEM(tokens.shape, BF16),
            pltpu.VMEM((rows, half), BF16),
            pltpu.VMEM((rows, half), BF16),
            pltpu.VMEM(a_t.shape, BF16),
            pltpu.VMEM(b_store.shape, BF16),
            pltpu.VMEM((8, 128), jnp.int32),
            pltpu.VMEM((2, 8, 128), jnp.int32),
            pltpu.VMEM((2, NZ, 64, 640), BF16),
            pltpu.VMEM((NZ, 64, 640), BF16),
            pltpu.VMEM((NZ, 32, 640), BF16),
            pltpu.VMEM((3, 32, 640), BF16),
            pltpu.VMEM((4, 32, 640), BF16),
            pltpu.VMEM((32, 640), BF16),
            pltpu.VMEM((2, NZ, 64, 640), BF16),
            pltpu.VMEM((64, half), BF16),
            pltpu.VMEM((64, cols), BF16),
            pltpu.VMEM((64, rows), F32),
            pltpu.VMEM((64, rows), F32),
            pltpu.VMEM((64, rows), BF16),
            pltpu.VMEM((heads, rows, rows), F32),
            pltpu.VMEM((heads, rows), F32),
            pltpu.VMEM((2, rows, rows), F32),
            pltpu.VMEM((rows, cols), F32),
            pltpu.VMEM((rows, cols), BF16),
            pltpu.VMEM((rows, cols), BF16),
            pltpu.VMEM((64, rows), F32),
            pltpu.VMEM((64, rows), F32),
            pltpu.VMEM((64, rows), BF16),
            pltpu.VMEM((4, rows, 1024), BF16),
            pltpu.VMEM((4, rows, 1024), BF16),
            pltpu.VMEM((rows, half), F32),
            pltpu.VMEM((rows, half), BF16),
            pltpu.VMEM((rows, half), BF16),
            pltpu.VMEM((2, NZ, 64, 640), BF16),
            pltpu.VMEM((NZ, 64, 640), BF16),
            pltpu.VMEM((3, 64, 640), BF16),
            pltpu.VMEM((4, 64, 640), BF16),
            pltpu.VMEM((64, 640), BF16),
            pltpu.VMEM((32, 640), BF16),
            pltpu.VMEM((32, 640), BF16),
            pltpu.VMEM((2, NZ, 64, 640), BF16),
            pltpu.VMEM(a_t.shape, BF16),
            pltpu.VMEM(b_store.shape, BF16),
            pltpu.SemaphoreType.DMA((SLOTS,)),
            pltpu.SemaphoreType.DMA((SLOTS,)),
            pltpu.SemaphoreType.DMA((10,)),
        ],
        compiler_params=pltpu.CompilerParams(
            collective_id=0, has_side_effects=True, vmem_limit_bytes=56 * 1024 * 1024
        ),
    )(
        block_slot, tenant_list, owner_slot, decay_rate, step_size.T,
        tokens, inner_x, grad_out, w_bc, a_t, b_store,
    )
    return mixed, igrad, jnp.swapaxes(agrad, 1, 2), bgrad


def solution(mesh):
    both = ("fsdp", "tenant")
    placed = (
        P(both, None),
        P(both, "tensor"),
        P(both, "tensor"),
        P("tensor"),
        P(both, "tensor"),
        P("fsdp", "tensor"),
        P(both, "tensor", None),
        P(both, None, "tensor"),
        P("tenant", None),
        P(both),
        P(),
    )
    return jax.shard_map(
        shards,
        mesh=mesh,
        in_specs=placed,
        out_specs=(
            P(both, "tensor"),
            P(both, "tensor"),
            P(both, "tensor", None),
            P(both, None, "tensor"),
        ),
        check_vma=False,
    )
```

```python
import jax
import jax.numpy as jnp
from jax import lax
from jax.experimental import pallas as pl
from jax.experimental.pallas import tpu as pltpu
from jax.sharding import PartitionSpec as P

MESH = pl.DeviceIdType.MESH
F32 = jnp.float32
BF16 = jnp.bfloat16
NZ = 8
HEADS_GRP = 32
NS = 256

X_, Z_, Y_, D_, XR = 0, 4, 36, 68, 84
LIST_, LOW, Q, PIN_ = 88, 90, 91, 92
CORE, ACROSS, Z1, Z2, OVER, GZ, GX, GC = 0, 1, 2, 5, 9, 10, 18, 26
FETCH, BACK = 96, 130
SLOTS = 164

NN = (((1,), (0,)), ((), ()))
NT = (((1,), (1,)), ((), ()))
TN = (((0,), (0,)), ((), ()))


def dot(a, b, dims=NN, precision=None):
    return lax.dot_general(a, b, dims, precision=precision, preferred_element_type=F32)


def body(
    slot_ref, list_ref, owner_ref, rate_ref, step_ref, tok_hbm, x_hbm, g_hbm, w_hbm, a_hbm, b_hbm,
    mixed_hbm, igrad_hbm, agrad_hbm, bgrad_hbm,
    w, tok, x, g, a_own, b_own, loc, listed, cand, rcore, rx, r1, r2, chunk, full,
    sel_a, sel_b, low_s, low_r, low_t, decay, tot, score_grad, acc, proj, gproj,
    q_s, q_r, q_t, psend, precv, part, mixed, igrad,
    bcand, brcore, br1, br2, bs, brx, bchunk, bfull, agrad, bgrad,
    ssem, rsem, lsem,
):
    f = lax.axis_index("fsdp")
    y = lax.axis_index("tenant")
    t = lax.axis_index("tensor")
    z = f // 4
    l = (f // 2) % 2
    c = f % 2
    p = y % 2
    rows = tok.shape[0]
    pairs = x.shape[1] // 128
    grp_pairs = pairs // 2

    def zat(d):
        return (z + d + NZ) % NZ

    def zdev(d):
        return (zat(d) * 4 + l * 2 + c, y, t)

    def ydev(d):
        return (f, (y + d + 4) % 4, t)

    sib = (z * 4 + l * 2 + (1 - c), y, t)
    xdev = (z * 4 + (1 - l) * 2 + c, y, t)
    tdev = (f, y, 1 - t)

    sent = []

    def send(src, dst, slot, dev):
        copy = pltpu.make_async_remote_copy(
            src_ref=src, dst_ref=dst, send_sem=ssem.at[slot], recv_sem=rsem.at[slot],
            device_id=dev, device_id_type=MESH,
        )
        copy.start()
        sent.append(copy)

    def got(dst, slot):
        pltpu.make_async_remote_copy(
            src_ref=dst, dst_ref=dst, send_sem=ssem.at[slot], recv_sem=rsem.at[slot],
            device_id=sib, device_id_type=MESH,
        ).wait_recv()

    def local(src, dst, slot):
        copy = pltpu.make_async_copy(src, dst, lsem.at[slot])
        copy.start()
        return copy

    def lside(which):
        return l if which == 0 else 1 - l

    def piece(d, which, par, h):
        first = pl.multiple_of((lside(which) * 2 + c) * 256 + par * 128 + h * 64, 64)
        return w.at[zat(d), pl.ds(first, 64), :]

    def move(part, slot, dev):
        send(part, part, slot, dev)

    def whole(d, which, core):
        first = pl.multiple_of((lside(which) * 2 + core) * 256, 256)
        return w.at[zat(d), pl.ds(first, 256), :]

    load_w = local(w_hbm, whole(0, 0, c), 0)
    load_a = local(a_hbm, a_own, 1)
    load_b = local(b_hbm, b_own, 2)
    load_x = local(x_hbm, x, 3)
    load_g = local(g_hbm, g, 4)
    load_tok = local(tok_hbm, tok, 5)

    barrier = pltpu.get_barrier_semaphore()
    partners = [sib, xdev, tdev] + [zdev(d) for d in range(1, NZ)] + [ydev(d) for d in range(1, 4)]
    for dev in partners:
        pl.semaphore_signal(barrier, inc=1, device_id=dev, device_id_type=MESH)
    pl.semaphore_wait(barrier, len(partners))

    loc[...] = jnp.where(
        lax.broadcasted_iota(jnp.int32, loc.shape, 0) == 0,
        owner_ref[list_ref[0, 0]],
        owner_ref[list_ref[0, 1]],
    )
    for j in range(2):
        send(loc, listed.at[j], LIST_ + j, ydev(2 - j))
    load_w.wait()
    for h in range(2):
        move(piece(0, 0, p, h), X_ + h, xdev)
        for way in range(2):
            move(piece(0, 0, p, h), Z_ + way * 16 + h, zdev(1 - 2 * way))
    send(whole(0, 0, c), whole(0, 0, c), D_, sib)

    upto = (
        lax.broadcasted_iota(jnp.int32, (rows, rows), 0)
        <= lax.broadcasted_iota(jnp.int32, (rows, rows), 1)
    ).astype(F32)
    tot[...] = dot(-step_ref[...], upto, precision=lax.Precision.HIGHEST)
    score_grad[...] = jnp.zeros_like(score_grad)
    acc[...] = jnp.zeros_like(acc)
    load_x.wait()
    load_g.wait()

    lanes = lax.broadcasted_iota(jnp.int32, (rows, 128), 1)

    def split_heads(values):
        wide = values.astype(F32)
        one = jnp.where(lanes < 64, wide, 0.0).astype(BF16)
        two = jnp.where(lanes >= 64, wide, 0.0).astype(BF16)
        return jnp.concatenate([one, two], axis=0)

    def decay_pairs(first, count):
        causal = lax.broadcasted_iota(jnp.int32, (rows, rows), 0) >= lax.broadcasted_iota(
            jnp.int32, (rows, rows), 1
        )

        def one_pair(k, carry):
            at = pl.multiple_of(k * 128, 128)
            both = split_heads(x[:, pl.ds(at, 128)])
            outer = dot(g[:, pl.ds(at, 128)], both, NT)
            total = jnp.zeros((rows, rows), F32)
            for i in range(2):
                head = 2 * k + i
                along = jnp.broadcast_to(tot[pl.ds(head, 1), :] * rate_ref[head], (rows, rows))
                spread = jnp.where(causal, along.T - along, -1e30)
                factor = jnp.exp(spread) * step_ref[pl.ds(head, 1), :]
                decay[head] = factor
                total += factor * outer[:, i * 128 : (i + 1) * 128]
            score_grad[k // grp_pairs] += total
            return carry

        lax.fori_loop(first, first + count, one_pair, 0)

    base = ((f * 4) + y) * 2
    for j in range(2):
        got(listed.at[j], LIST_ + j)

    def picked(j, k):
        return (listed[j, j : j + 1, :] == base + k).astype(F32)

    load_a.wait()
    load_b.wait()
    for j in range(2):
        m0, m1 = picked(j, 0), picked(j, 1)
        for zc in range(NZ):
            for i in range(5):
                src, at = (a_own, zc * 512 + i * 128) if i < 4 else (b_own, zc * 128)
                value = (
                    src[0, :, at : at + 128].astype(F32) * m0
                    + src[1, :, at : at + 128].astype(F32) * m1
                )
                cand[j, zc, :, i * 128 : (i + 1) * 128] = value.astype(BF16)
    send(cand.at[1 - c], rcore, FETCH + CORE, sib)
    mine = pl.ds(pl.multiple_of(32 * l, 32), 32)
    other = pl.ds(pl.multiple_of(32 * (1 - l), 32), 32)

    turn = 1 - 2 * c

    def zturn(d):
        return zat(turn * d)

    def zway(d):
        return zdev(turn * d)

    def reduce_start(own, one, two, at):
        send(own(3), one.at[0], at + Z1, zway(1))
        send(own(4), one.at[1], at + Z1 + 1, zway(2))
        send(own(-3), one.at[2], at + Z1 + 2, zway(-1))
        send(own(1), two.at[0], at + Z2, zway(1))
        send(own(-1), two.at[1], at + Z2 + 1, zway(-1))

    def reduce_relay(own, one, two, at):
        for i in range(3):
            got(one.at[i], at + Z1 + i)
        up = one[0].astype(F32) + one[1].astype(F32) + own(2)[...].astype(F32)
        one[0] = up.astype(BF16)
        send(one.at[0], two.at[2], at + Z2 + 2, zway(2))
        one[2] = (one[2].astype(F32) + own(-2)[...].astype(F32)).astype(BF16)
        send(one.at[2], two.at[3], at + Z2 + 3, zway(-2))

    def reduce_end(own, two, at):
        total = own(0)[...].astype(F32)
        for i in range(4):
            got(two.at[i], at + Z2 + i)
            total += two[i].astype(F32)
        return total

    def held(buf, d, wide):
        return buf.at[c, zturn(-d)] if wide else buf.at[c, zturn(-d), mine, :]

    def gather_start(buf, at, wide):
        own = held(buf, 0, wide)
        for d in (2, -2, 1, -1):
            move(own, at + GZ + d % 8, zway(d))
        move(own, at + (GC if wide else GX), sib if wide else xdev)

    def gather_in(buf, at, wide, d, hops=()):
        here = held(buf, d, wide)
        got(here, at + GZ + d % 8)
        for hop in hops:
            move(here, at + GZ + (d + hop) % 8, zway(hop))
        move(here, at + (GC if wide else GX) + d % 8, sib if wide else xdev)

    def gather_core(buf, at, offs):
        for d in offs:
            got(buf.at[c, zturn(-d), other, :], at + GX + d % 8)
            send(buf.at[c, zturn(-d)], buf.at[c, zturn(-d)], at + GC + d % 8, sib)

    def gather_end(buf, at, offs):
        for d in offs:
            got(buf.at[1 - c, zturn(d)], at + GC + d % 8)


    def zstep(s, side):
        for h in range(2):
            for way, which, last in ((0, 0, 4), (1, 0, 2), (1, 1, 4), (0, 1, 2)):
                if s > last or which != side:
                    continue
                d = -s if way == 0 else s
                slot = Z_ + way * 16 + which * 8 + (s - 1) * 2 + h
                part_in = piece(d, which, p, h)
                got(part_in, slot)
                if s < last:
                    move(part_in, slot + 2, zdev(1 - 2 * way))
                move(part_in, Y_ + which * 16 + d % 8 * 2 + h, ydev(1 if which == 0 else -1))
                if s == 3:
                    move(part_in, XR + way * 2 + h, xdev)

    def xstep(way):
        d, which = (-3, 1) if way == 0 else (3, 0)
        for h in range(2):
            part_in = piece(d, which, p, h)
            got(part_in, XR + way * 2 + h)
            move(part_in, Y_ + which * 16 + d % 8 * 2 + h, ydev(1 if which == 0 else -1))

    def offsets(s):
        return (0,) if s == 0 else (4,) if s == 4 else (-s, s)

    def ystep(s):
        for d in offsets(s):
            for which in range(2):
                for h in range(2):
                    got(piece(d, which, 1 - p, h), Y_ + which * 16 + d % 8 * 2 + h)
                send(whole(d, which, c), whole(d, which, c), D_ + which * 8 + d % 8, sib)

    def forward(s):
        for d in offsets(s):
            for which in range(2):
                got(whole(d, which, 1 - c), D_ + which * 8 + d % 8)
        for d in offsets(s):
            at = zat(d)

            def part_n(n, carry, at=at):
                cols = pl.ds(pl.multiple_of(n * 256, 256), 256)
                acc[:, cols] += dot(
                    tok[:, pl.ds(pl.multiple_of(at * 1024, 1024), 1024)], w[at, :, cols]
                )
                return carry

            lax.fori_loop(0, 4, part_n, 0)

    quarter = pairs // 4

    def own_rows(k):
        return rx.at[zturn(k)]

    for h in range(2):
        got(piece(0, 1, p, h), X_ + h)
        for way in range(2):
            move(piece(0, 1, p, h), Z_ + way * 16 + 8 + h, zdev(1 - 2 * way))
    got(rcore, FETCH + CORE)
    cand[c] = cand[c] + rcore[...]
    send(cand.at[c, :, other, :], rx, FETCH + ACROSS, xdev)
    zstep(1, 0)
    zstep(1, 1)
    decay_pairs(0, quarter * 2)
    got(rx, FETCH + ACROSS)
    rx[...] = rx[...] + cand[c, :, mine, :]
    reduce_start(own_rows, r1, r2, FETCH)
    zstep(2, 0)
    for h in range(2):
        move(piece(0, 0, 1 - p, h), X_ + 2 + h, xdev)
    decay_pairs(quarter * 2, quarter)
    ystep(1)
    zstep(2, 1)
    load_tok.wait()
    forward(1)
    reduce_relay(own_rows, r1, r2, FETCH)
    zstep(3, 0)
    zstep(3, 1)
    chunk[...] = reduce_end(own_rows, r2, FETCH).astype(BF16)
    send(chunk, full.at[c, z, mine, :], FETCH + OVER, ydev(2 + c))
    for h in range(2):
        got(piece(0, 1, 1 - p, h), X_ + 2 + h)
    send(whole(0, 1, c), whole(0, 1, c), D_ + 8, sib)
    ystep(2)
    decay_pairs(quarter * 3, quarter // 2)
    xstep(0)
    forward(0)
    got(full.at[c, z, mine, :], FETCH + OVER)
    gather_start(full, FETCH, False)
    zstep(4, 1)
    xstep(1)
    gather_in(full, FETCH, False, 2, (1, 2))
    gather_in(full, FETCH, False, -2, (-1,))
    zstep(4, 0)
    forward(2)
    ystep(3)
    for d in (1, -1, 3, -3, 4):
        gather_in(full, FETCH, False, d)
    decay_pairs(quarter * 3 + quarter // 2, quarter // 2)
    forward(3)
    gather_core(full, FETCH, (0, 2, -2, 1, -1, 3, -3, 4))
    ystep(4)
    gather_end(full, FETCH, range(NZ))
    slot = slot_ref[0]
    half = pl.multiple_of(t * 4096, 4096)
    low_part = jnp.zeros((64, rows), F32)
    for zc in range(NZ):
        piece_ab = full[slot, zc]
        sel_a[:, zc * 512 : (zc + 1) * 512] = piece_ab[:, :512]
        sel_b[:, zc * 128 : (zc + 1) * 128] = piece_ab[:, 512:]
        low_part += dot(piece_ab[:, :512], tok[:, pl.ds(half + zc * 512, 512)], NT)
    low_s[...] = low_part
    send(low_s, low_r, LOW, tdev)
    forward(4)
    got(low_r, LOW)
    low_t[...] = (low_s[...] + low_r[...]).astype(BF16)
    proj[...] = (acc[...] + dot(low_t[...], sel_b[...], TN)).astype(BF16)

    for gi in range(2):
        b_in = proj[:, gi * 512 : gi * 512 + 256]
        c_out = proj[:, gi * 512 + 256 : gi * 512 + 512]
        sg = score_grad[gi].astype(BF16)
        gproj[:, gi * 512 : gi * 512 + 256] = dot(sg, c_out, TN).astype(BF16)
        gproj[:, gi * 512 + 256 : gi * 512 + 512] = dot(sg, b_in).astype(BF16)
    q_s[...] = dot(sel_b[...], gproj[...], NT)
    send(q_s, q_r, Q, tdev)
    for gi in range(2):
        c_out = proj[:, gi * 512 + 256 : gi * 512 + 512]
        score_grad[gi] = dot(c_out, proj[:, gi * 512 : gi * 512 + 256], NT)

    def back(at, n):
        return dot(gproj[...], w[at, pl.ds(pl.multiple_of(n * 256, 256), 256), :], NT)

    def partner(k):
        def partner_n(n, carry):
            cols = pl.ds(pl.multiple_of(n * 256, 256), 256)
            psend[k, :, cols] = back(4 * (1 - t) + k, n).astype(BF16)
            return carry

        lax.fori_loop(0, 4, partner_n, 0)

    def to_partner(k):
        send(psend.at[k], precv.at[k], PIN_ + k, tdev)

    partner(0)
    to_partner(0)

    got(q_r, Q)
    q_t[...] = (q_s[...] + q_r[...]).astype(BF16)
    for zc in range(NZ):
        ga = dot(q_t[...], tok[:, pl.ds(half + zc * 512, 512)])
        gb = dot(low_t[...], gproj[:, zc * 128 : (zc + 1) * 128])
        for j in range(2):
            chosen = jnp.where(slot == j, 1.0, 0.0).astype(F32)
            bcand[j, zc, :, :512] = (ga * chosen).astype(BF16)
            bcand[j, zc, :, 512:] = (gb * chosen).astype(BF16)
    send(bcand.at[1 - c], brcore, BACK + CORE, sib)
    partner(1)
    to_partner(1)

    def own_n(n, carry):
        cols = pl.ds(pl.multiple_of(n * 256, 256), 256)
        part[:, cols] = back(4 * t + n // 4, n % 4) + dot(q_t[...], sel_a[:, cols], TN)
        return carry

    def own_sum(k):
        return bcand.at[c, zturn(k)]

    got(brcore, BACK + CORE)
    for zc in range(NZ):
        bcand[c, zc] = (bcand[c, zc].astype(F32) + brcore[zc].astype(F32)).astype(BF16)
    reduce_start(own_sum, br1, br2, BACK)
    partner(2)
    to_partner(2)
    partner(3)
    to_partner(3)
    lax.fori_loop(0, 5, own_n, 0)
    reduce_relay(own_sum, br1, br2, BACK)
    lax.fori_loop(5, 16, own_n, 0)

    def mix_pair(k, carry):
        at = pl.multiple_of(k * 128, 128)
        both = split_heads(x[:, pl.ds(at, 128)])
        score = score_grad[k // grp_pairs]
        weight = jnp.concatenate(
            [(decay[2 * k] * score).astype(BF16), (decay[2 * k + 1] * score).astype(BF16)], axis=1
        )
        mixed[:, pl.ds(at, 128)] = dot(weight, both).astype(BF16)
        return carry

    bs[...] = reduce_end(own_sum, br2, BACK).astype(BF16)
    send(bs.at[other, :], brx, BACK + ACROSS, xdev)
    got(brx, BACK + ACROSS)
    bchunk[...] = (bs[mine, :].astype(F32) + brx[...].astype(F32)).astype(BF16)
    send(bchunk, bfull.at[c, z, mine, :], BACK + OVER, ydev(2 - c))
    lax.fori_loop(0, pairs // 4, mix_pair, 0)
    got(bfull.at[c, z, mine, :], BACK + OVER)
    gather_start(bfull, BACK, False)
    lax.fori_loop(pairs // 4, pairs // 2, mix_pair, 0)
    gather_in(bfull, BACK, False, 2, (1, 2))
    gather_in(bfull, BACK, False, -2, (-1,))
    lax.fori_loop(pairs // 2, pairs, mix_pair, 0)
    out_mixed = local(mixed, mixed_hbm, 6)

    def total_k(k):
        got(precv.at[k], PIN_ + k)
        cols = slice(k * 1024, (k + 1) * 1024)
        igrad[:, cols] = (part[:, cols] + precv[k].astype(F32)).astype(BF16)

    masks = [[picked(j, k) for j in range(2)] for k in range(2)]

    def place(offs):
        for d in offs:
            at = zat(d)
            for k in range(2):
                for i in range(5):
                    dst, first = (agrad, at * 512 + i * 128) if i < 4 else (bgrad, at * 128)
                    lane = slice(i * 128, (i + 1) * 128)
                    value = (
                        bfull[0, at, :, lane].astype(F32) * masks[k][0]
                        + bfull[1, at, :, lane].astype(F32) * masks[k][1]
                    )
                    dst[k, :, pl.ds(pl.multiple_of(first, 128), 128)] = value.astype(BF16)

    for d in (1, -1):
        gather_in(bfull, BACK, False, d)
    total_k(0)
    total_k(1)
    gather_core(bfull, BACK, (0, 2, -2, 1, -1))
    for d in (3, -3, 4):
        gather_in(bfull, BACK, False, d)
    total_k(2)
    gather_core(bfull, BACK, (3, -3, 4))
    gather_end(bfull, BACK, (0, 1, -1, 2, -2))
    place((0, 1, -1, 2, -2))
    gather_end(bfull, BACK, (3, -3, 4))
    place((3, -3, 4))
    out_a = local(agrad, agrad_hbm, 8)
    total_k(3)
    out_igrad = local(igrad, igrad_hbm, 7)
    out_b = local(bgrad, bgrad_hbm, 9)
    for copy in sent:
        copy.wait_send()
    for copy in (out_mixed, out_igrad, out_a, out_b):
        copy.wait()


def shards(
    tokens, inner_x, step_size, decay_rate, grad_out, w_bc,
    a_store, b_store, tenant_list, block_slot, owner_slot,
):
    rows = tokens.shape[0]
    heads = decay_rate.shape[0]
    a_t = jnp.swapaxes(a_store, 1, 2)
    half = inner_x.shape[1]
    cols = w_bc.shape[1]
    hbm = pl.BlockSpec(memory_space=pltpu.HBM)
    free = pl.BlockSpec(memory_space=pl.ANY)
    vmem = pl.BlockSpec(memory_space=pltpu.VMEM)
    smem = pl.BlockSpec(memory_space=pltpu.SMEM)
    mixed, igrad, agrad, bgrad = pl.pallas_call(
        body,
        out_shape=(
            jax.ShapeDtypeStruct((rows, half), BF16),
            jax.ShapeDtypeStruct((rows, half), BF16),
            jax.ShapeDtypeStruct(a_t.shape, BF16),
            jax.ShapeDtypeStruct(b_store.shape, BF16),
        ),
        in_specs=[smem, smem, smem, smem, vmem, hbm, hbm, hbm, hbm, hbm, hbm],
        out_specs=(free, free, free, free),
        scratch_shapes=[
            pltpu.VMEM((NZ, 1024, cols), BF16),
            pltpu.VMEM(tokens.shape, BF16),
            pltpu.VMEM((rows, half), BF16),
            pltpu.VMEM((rows, half), BF16),
            pltpu.VMEM(a_t.shape, BF16),
            pltpu.VMEM(b_store.shape, BF16),
            pltpu.VMEM((8, 128), jnp.int32),
            pltpu.VMEM((2, 8, 128), jnp.int32),
            pltpu.VMEM((2, NZ, 64, 640), BF16),
            pltpu.VMEM((NZ, 64, 640), BF16),
            pltpu.VMEM((NZ, 32, 640), BF16),
            pltpu.VMEM((3, 32, 640), BF16),
            pltpu.VMEM((4, 32, 640), BF16),
            pltpu.VMEM((32, 640), BF16),
            pltpu.VMEM((2, NZ, 64, 640), BF16),
            pltpu.VMEM((64, half), BF16),
            pltpu.VMEM((64, cols), BF16),
            pltpu.VMEM((64, rows), F32),
            pltpu.VMEM((64, rows), F32),
            pltpu.VMEM((64, rows), BF16),
            pltpu.VMEM((heads, rows, rows), F32),
            pltpu.VMEM((heads, rows), F32),
            pltpu.VMEM((2, rows, rows), F32),
            pltpu.VMEM((rows, cols), F32),
            pltpu.VMEM((rows, cols), BF16),
            pltpu.VMEM((rows, cols), BF16),
            pltpu.VMEM((64, rows), F32),
            pltpu.VMEM((64, rows), F32),
            pltpu.VMEM((64, rows), BF16),
            pltpu.VMEM((4, rows, 1024), BF16),
            pltpu.VMEM((4, rows, 1024), BF16),
            pltpu.VMEM((rows, half), F32),
            pltpu.VMEM((rows, half), BF16),
            pltpu.VMEM((rows, half), BF16),
            pltpu.VMEM((2, NZ, 64, 640), BF16),
            pltpu.VMEM((NZ, 64, 640), BF16),
            pltpu.VMEM((3, 64, 640), BF16),
            pltpu.VMEM((4, 64, 640), BF16),
            pltpu.VMEM((64, 640), BF16),
            pltpu.VMEM((32, 640), BF16),
            pltpu.VMEM((32, 640), BF16),
            pltpu.VMEM((2, NZ, 64, 640), BF16),
            pltpu.VMEM(a_t.shape, BF16),
            pltpu.VMEM(b_store.shape, BF16),
            pltpu.SemaphoreType.DMA((SLOTS,)),
            pltpu.SemaphoreType.DMA((SLOTS,)),
            pltpu.SemaphoreType.DMA((10,)),
        ],
        compiler_params=pltpu.CompilerParams(
            collective_id=0, has_side_effects=True, vmem_limit_bytes=56 * 1024 * 1024
        ),
    )(
        block_slot, tenant_list, owner_slot, decay_rate, step_size.T,
        tokens, inner_x, grad_out, w_bc, a_t, b_store,
    )
    return mixed, igrad, jnp.swapaxes(agrad, 1, 2), bgrad


def solution(mesh):
    both = ("fsdp", "tenant")
    placed = (
        P(both, None),
        P(both, "tensor"),
        P(both, "tensor"),
        P("tensor"),
        P(both, "tensor"),
        P("fsdp", "tensor"),
        P(both, "tensor", None),
        P(both, None, "tensor"),
        P("tenant", None),
        P(both),
        P(),
    )
    return jax.shard_map(
        shards,
        mesh=mesh,
        in_specs=placed,
        out_specs=(
            P(both, "tensor"),
            P(both, "tensor"),
            P(both, "tensor", None),
            P(both, None, "tensor"),
        ),
        check_vma=False,
    )
```
